256 devices in a mesh: gx: 8 (over y_hi, x), gy: 32 (over y_lo, z, core).
Axes of the slice: x: 4, y: 4 (y_hi: 2, y_lo: 2; y = y_hi * 2 + y_lo), z: 8, core: 2. Of those that a mesh axis runs over, the one named last changes fastest.
Arguments:
- white_noise: float32 [2, 32, 1024, 1024], P(None, None, 'gy', 'gx'), may hold values from -6 to 6
- head_start: float32 [2, 32, 1024, 1024], P(None, None, 'gy', 'gx'), may hold values from -6 to 6
Outputs:
- log_conductivity: float32 [2, 32, 1024, 1024], P(None, None, 'gy', 'gx')
- hydraulic_head: float32 [2, 32, 1024, 1024], P(None, None, 'gy', 'gx')
The draws below stay inside these ranges and needn't reach their ends.
All inputs are finite; a program needn't handle non-finite values.
Results may differ from the reference program's by a relative error of at most 0.0001.
Values sent between devices are 32-bit elements; how exact they have to be, the bound alone decides.
A program may use at most 64 MiB of HBM per device.

```python
import math
import jax
import jax.numpy as jnp
from jax import lax

NX = 1024
NY = 1024
NZ = 32
MEMBERS = 2
SWEEPS = 2


def block_scale(stream_key, shape, split, smallest, top_value):
    gain, own = 1.0, jax.random.fold_in(stream_key, 6)
    for dim, shards_of in split:
        steps = jnp.exp(jax.random.uniform(jax.random.fold_in(own, dim), (shards_of,), jnp.float32, smallest / len(split), top_value / len(split)))
        gain = gain * jnp.repeat(steps, shape[dim] // shards_of).reshape([-1 if axis == dim else 1 for axis in range(len(shape))])
    return gain


def centred(stream_key, shape, deviation, most, split=(), held_as=jnp.bfloat16):
    drawn = deviation * jax.random.normal(stream_key, shape, jnp.float32)
    if split:
        drawn = drawn * block_scale(stream_key, shape, split, -0.22, 0.18)
    return jnp.clip(drawn, -most, most).astype(held_as)


def setup_inputs(seed: int = 0) -> dict:
    seeds = jax.random.split(jax.random.key(seed), 3)
    return {
        "white_noise": centred(seeds[0], (MEMBERS, NZ, NY, NX), 1.0, 6.0, ((2, 32), (3, 8)), jnp.float32),
        "head_start": centred(seeds[1], (MEMBERS, NZ, NY, NX), 1.0, 6.0, ((2, 32), (3, 8)), jnp.float32),
    }


TWO_PI = 2.0 * math.pi

def axis_amplitude(length):
    wave_index = jnp.arange(length, dtype=jnp.int32)
    folded = jnp.minimum(wave_index, length - wave_index).astype(jnp.float32)
    wavenumber = TWO_PI * folded / length
    corr_length = length / 16.0
    spectrum = 1.0 / (1.0 + wavenumber * corr_length * (wavenumber * corr_length))
    return jnp.sqrt(spectrum / jnp.mean(spectrum))

def boundary_mask(layer_count, row_count, col_count, row_start, col_start):
    shape = (layer_count, row_count, col_count)
    layer_index = lax.broadcasted_iota(jnp.int32, shape, 0)
    row_glob = row_start + lax.broadcasted_iota(jnp.int32, shape, 1)
    col_glob = col_start + lax.broadcasted_iota(jnp.int32, shape, 2)
    return (layer_index == 0) | (layer_index == NZ - 1) | (row_glob <= 0) | (row_glob >= NY - 1) | (col_glob <= 0) | (col_glob >= NX - 1)

def relax(head_ext, cond_ext, pinned):
    head_mid = head_ext[..., 1:-1, 1:-1]
    cond_mid = cond_ext[..., 1:-1, 1:-1]
    pad_layers = ((0, 0), (1, 1), (0, 0), (0, 0))
    head_zpad = jnp.pad(head_mid, pad_layers)
    cond_zpad = jnp.pad(cond_mid, pad_layers, constant_values=1.0)
    neighbours = [(head_ext[..., 1:-1, 2:], cond_ext[..., 1:-1, 2:]), (head_ext[..., 1:-1, :-2], cond_ext[..., 1:-1, :-2]), (head_ext[..., 2:, 1:-1], cond_ext[..., 2:, 1:-1]), (head_ext[..., :-2, 1:-1], cond_ext[..., :-2, 1:-1]), (head_zpad[:, 2:], cond_zpad[:, 2:]), (head_zpad[:, :-2], cond_zpad[:, :-2])]
    weighted = jnp.zeros_like(head_mid)
    total_weight = jnp.zeros_like(head_mid)
    for head_nb, cond_nb in neighbours:
        coupling = 2.0 * cond_mid * cond_nb / (cond_mid + cond_nb)
        weighted = weighted + coupling * head_nb
        total_weight = total_weight + coupling
    return jnp.where(pinned, head_mid, weighted / total_weight)

def reference(white_noise, head_start):
    amplitude = axis_amplitude(NZ)[:, None, None] * axis_amplitude(NY)[None, :, None] * axis_amplitude(NX)[None, None, :]
    fields = []
    for member in range(MEMBERS):
        spectral = jnp.fft.fftn(white_noise[member]) * amplitude
        fields.append(jnp.real(jnp.fft.ifftn(spectral)).astype(jnp.float32))
    log_conductivity = jnp.stack(fields)
    conductivity = jnp.exp(log_conductivity)
    pinned = boundary_mask(NZ, NY, NX, 0, 0)
    cond_ext = jnp.pad(conductivity, ((0, 0), (0, 0), (1, 1), (1, 1)), constant_values=1.0)
    head = head_start
    for sweep_index in range(SWEEPS):
        head = relax(jnp.pad(head, ((0, 0), (0, 0), (1, 1), (1, 1))), cond_ext, pinned)
    return (log_conductivity, head)
```

```python
import functools
import math

import jax
import jax.numpy as jnp
import ml_dtypes
import numpy as np
from jax import lax
from jax.experimental import pallas as pl
from jax.experimental.pallas import tpu as pltpu
from jax.sharding import PartitionSpec as P

F32 = jnp.float32
BF16 = jnp.bfloat16
MESH = pl.DeviceIdType.MESH
PAD = 8


def circulant(length):
    k = np.arange(length)
    q = np.minimum(k, length - k)
    w = 2.0 * math.pi * q / length
    s = 1.0 / (1.0 + (w * (length / 16.0)) ** 2)
    a = np.sqrt(s / np.mean(s))
    taps = np.real(np.fft.ifft(a))
    return taps[(k[:, None] - k[None, :]) % length]


def split_pair(matrix):
    high = matrix.astype(ml_dtypes.bfloat16)
    low = (matrix - high.astype(np.float64)).astype(ml_dtypes.bfloat16)
    return np.stack([high, low])


def split(x):
    high = x.astype(BF16)
    low = (x - high.astype(F32)).astype(BF16)
    return high, low


def dot(a, b):
    return jnp.dot(a, b, preferred_element_type=F32)


def line_of(gx, gy, i, j):
    if (gx, gy) == (8, 32):
        core, z, y_lo = j % 2, (j // 2) % 8, j // 16
        x, y_hi = i % 4, i // 4
        t = z % 4
        x_to = (x + t % 2 + 2 * core) % 4
        y_to = (y_hi + core + t // 2) % 2
        return y_lo * 2 + z // 4, y_to * 4 + x_to
    return j // gx, (j % gx + i) % gx


def body(
    gx, gy, n, nz, yb, xb,
    w_hbm, h_hbm, c_hbm, kz_hbm, lk_hbm, ho_hbm,
    w_v, c_v, kz_v, zc, r1, acat, xo, r2, bcat, yo, lk,
    hb, rb, gb, wt, ho, row_out, row_in, col_out, col_in,
    in_sem, c_sem, s1, v1, s2, v2, s3, v3, hs, hv, out_sem,
):
    i = lax.axis_index("gx")
    j = lax.axis_index("gy")
    zc_n = nz // gx
    wide = yb + 2 * PAD
    rows = zc_n * yb
    members = range(2)

    w_in = [pltpu.make_async_copy(w_hbm.at[m], w_v.at[m], in_sem.at[m]) for m in members]
    h_in = [
        pltpu.make_async_copy(
            h_hbm.at[m], hb.at[m, :, pl.ds(PAD, yb)], in_sem.at[2 + m]
        )
        for m in members
    ]
    kz_in = pltpu.make_async_copy(kz_hbm, kz_v, c_sem.at[0])
    c_in = pltpu.make_async_copy(c_hbm, c_v, c_sem.at[1])
    kz_in.start()
    w_in[0].start()
    w_in[1].start()
    h_in[0].start()
    h_in[1].start()
    c_in.start()

    barrier = pltpu.get_barrier_semaphore()

    @pl.loop(1, gx)
    def _(k):
        pl.semaphore_signal(barrier, inc=1, device_id=((i + k) % gx, j), device_id_type=MESH)

    @pl.loop(1, gy)
    def _(k):
        pl.semaphore_signal(barrier, inc=1, device_id=(i, (j + k) % gy), device_id_type=MESH)

    def filter_z(m):
        for q in range(yb // 8):
            x = w_v[m, :, 8 * q : 8 * q + 8, :].reshape(nz * 8, xb)
            high, low = split(x)
            p = dot(kz_v[0], jnp.concatenate([high, low], axis=1))
            r = p[:, :xb] + p[:, xb:] + dot(kz_v[1], high)
            zc[m, :, 8 * q : 8 * q + 8, :] = r.reshape(nz, 8, xb)
        r1[m, i] = zc[m, pl.ds(zc_n * i, zc_n)]

    def copy1(m, peer):
        return pltpu.make_async_remote_copy(
            src_ref=zc.at[m, pl.ds(zc_n * peer, zc_n)],
            dst_ref=r1.at[m, i],
            send_sem=s1.at[m],
            recv_sem=v1.at[m],
            device_id=(peer, j),
            device_id_type=MESH,
        )

    def send1(m):
        @pl.loop(1, gx)
        def _(k):
            copy1(m, (i + k) % gx).start()

    kz_in.wait()
    w_in[0].wait()
    filter_z(0)
    pl.semaphore_wait(barrier, gx + gy - 2)
    send1(0)
    w_in[1].wait()
    filter_z(1)
    send1(1)

    lane = lax.broadcasted_iota(jnp.int32, (yb, xb), 1)
    peers = (
        ((i + gx - 1) % gx, j),
        ((i + 1) % gx, j),
        (i, (j + gy - 1) % gy),
        (i, (j + 1) % gy),
    )

    def edge_copy(field, m, side):
        out, inn = (col_out, col_in) if side < 2 else (row_out, row_in)
        return pltpu.make_async_remote_copy(
            src_ref=out.at[field, m, side % 2],
            dst_ref=inn.at[field, m, side % 2],
            send_sem=hs.at[field, m, side],
            recv_sem=hv.at[field, m, side],
            device_id=peers[side],
            device_id_type=MESH,
        )

    def send_edges(field, ref, m):
        for z in range(nz):
            row_out[field, m, 0, z : z + 1, :] = ref[m, z, PAD : PAD + 1, :]
            row_out[field, m, 1, z : z + 1, :] = ref[m, z, PAD + yb - 1 : PAD + yb, :]
        edge_copy(field, m, 2).start()
        edge_copy(field, m, 3).start()

        def pack(z, carry):
            to_left, to_right = carry
            x = ref[m, z, PAD : PAD + yb, :]
            left_at = (2 * z + xb - 1) % xb
            to_left = jnp.where(lane == left_at, pltpu.roll(x, left_at, 1), to_left)
            to_right = jnp.where(lane == 2 * z, pltpu.roll(x, 2 * z + 1, 1), to_right)
            return to_left, to_right

        zero = jnp.zeros((yb, xb), F32)
        to_left, to_right = lax.fori_loop(0, nz, pack, (zero, zero), unroll=4)
        col_out[field, m, 0] = to_left
        col_out[field, m, 1] = to_right
        edge_copy(field, m, 0).start()
        edge_copy(field, m, 1).start()

    def take_edges(field, ref, m):
        for side in range(4):
            edge_copy(field, m, side).wait_recv()
        for z in range(nz):
            ref[m, z, PAD + yb : PAD + yb + 1, :] = row_in[field, m, 0, z : z + 1, :]
            ref[m, z, PAD - 1 : PAD, :] = row_in[field, m, 1, z : z + 1, :]
        return jnp.where(lane % 2 == 0, col_in[field, m, 1], col_in[field, m, 0])

    for m in members:
        h_in[m].wait()
        send_edges(0, hb, m)

    def wait_all(ref, sem):
        pltpu.make_async_copy(ref, ref, sem).wait()

    def copy2(m, k):
        jp = (j + k) % gy
        a, xe = line_of(gx, gy, i, jp)
        return pltpu.make_async_remote_copy(
            src_ref=xo.at[m, xe, pl.ds(yb * a, yb)],
            dst_ref=r2.at[m, j],
            send_sem=s2.at[m],
            recv_sem=v2.at[m],
            device_id=(i, jp),
            device_id_type=MESH,
        )

    my_a, my_xe = line_of(gx, gy, i, j)

    def filter_x(m):
        for s in range(gx):
            high, low = split(r1[m, s].reshape(rows, xb))
            acat[0:rows, s * xb : (s + 1) * xb] = high
            acat[rows : 2 * rows, s * xb : (s + 1) * xb] = low
        for c in range(n // (2 * xb)):
            cols = slice(2 * xb * c, 2 * xb * (c + 1))
            p = dot(acat[...], c_v[0, :, cols])
            r = p[:rows] + p[rows:] + dot(acat[0:rows, :], c_v[1, :, cols])
            xo[m, 2 * c] = r[:, :xb]
            xo[m, 2 * c + 1] = r[:, xb:]
        r2[m, j] = xo[m, my_xe, pl.ds(yb * my_a, yb), :]

    c_in.wait()
    for m in members:
        wait_all(r1.at[m, pl.ds(0, gx - 1)], v1.at[m])
        filter_x(m)

        @pl.loop(1, gy)
        def _(k):
            copy2(m, k).start()

    my_z = zc_n * i + my_a

    def copy3(m, jp):
        return pltpu.make_async_remote_copy(
            src_ref=yo.at[m, jp],
            dst_ref=lk.at[m, my_z],
            send_sem=s3.at[m],
            recv_sem=v3.at[m],
            device_id=(my_xe, jp),
            device_id_type=MESH,
        )

    def keep3(m):
        return pltpu.make_async_copy(yo.at[m, j], lk.at[m, my_z], v3.at[m])

    def filter_y(m):
        per = 256 // yb
        for s in range(gy):
            high, low = split(r2[m, s])
            bcat[s * yb : (s + 1) * yb, 0:xb] = high
            bcat[s * yb : (s + 1) * yb, xb : 2 * xb] = low
        for c in range(n // 256):
            lines = slice(256 * c, 256 * (c + 1))
            p = dot(c_v[0, lines, :], bcat[...])
            r = p[:, :xb] + p[:, xb:] + dot(c_v[1, lines, :], bcat[:, 0:xb])
            yo[m, per * c : per * (c + 1)] = r.reshape(per, yb, xb)

    for m in members:
        wait_all(r2.at[m, pl.ds(0, gy - 1)], v2.at[m])
        filter_y(m)

        @pl.when(my_xe != i)
        def _():
            copy3(m, j).start()

        @pl.when(my_xe == i)
        def _():
            keep3(m).start()

        @pl.loop(1, gy)
        def _(k):
            copy3(m, (j + k) % gy).start()

    row_at = yb * j + lax.broadcasted_iota(jnp.int32, (yb, xb), 0)
    col_at = xb * i + lane
    pinned = (row_at == 0) | (row_at == n - 1) | (col_at == 0) | (col_at == n - 1)

    def sides(ref, m, z, edge):
        x = ref[m, z, PAD : PAD + yb, :]
        e = pltpu.roll(edge, (xb - 2 * z) % xb, 1)
        left = jnp.where(lane == 0, e, pltpu.roll(x, 1, 1))
        right = jnp.where(lane == xb - 1, e, pltpu.roll(x, xb - 1, 1))
        up = ref[m, z, PAD - 1 : PAD - 1 + yb, :]
        down = ref[m, z, PAD + 1 : PAD + 1 + yb, :]
        below = ref[m, z - 1, PAD : PAD + yb, :]
        above = ref[m, z + 1, PAD : PAD + yb, :]
        return x, (left, right, up, down, below, above)

    for m in members:
        wait_all(lk.at[m], v3.at[m])
        pltpu.make_async_copy(lk.at[m], lk_hbm.at[m], out_sem.at[m]).start()

        @pl.loop(0, nz)
        def _(z):
            rb[m, z, PAD : PAD + yb, :] = jnp.exp(-lk[m, z])

        send_edges(1, rb, m)
        h_edge = take_edges(0, hb, m)
        r_edge = take_edges(1, rb, m)

        gb[m, 0, PAD : PAD + yb, :] = hb[m, 0, PAD : PAD + yb, :]
        gb[m, nz - 1, PAD : PAD + yb, :] = hb[m, nz - 1, PAD : PAD + yb, :]
        ho[m, 0] = hb[m, 0, PAD : PAD + yb, :]
        ho[m, nz - 1] = hb[m, nz - 1, PAD : PAD + yb, :]

        @pl.loop(1, nz - 1)
        def _(z):
            r, r_sides = sides(rb, m, z, r_edge)
            h, h_sides = sides(hb, m, z, h_edge)
            weights = [1.0 / (r + r_side) for r_side in r_sides]
            total = sum(weights[1:], weights[0])
            inverse = 1.0 / total
            new = jnp.zeros_like(h)
            for d in range(6):
                weight = weights[d] * inverse
                wt[z, d] = weight
                new = new + weight * h_sides[d]
            gb[m, z, PAD : PAD + yb, :] = jnp.where(pinned, h, new)

        send_edges(2, gb, m)
        g_edge = take_edges(2, gb, m)

        @pl.loop(1, nz - 1)
        def _(z):
            h, h_sides = sides(gb, m, z, g_edge)
            new = jnp.zeros_like(h)
            for d in range(6):
                new = new + wt[z, d] * h_sides[d]
            ho[m, z] = jnp.where(pinned, h, new)

        pltpu.make_async_copy(ho.at[m], ho_hbm.at[m], out_sem.at[2 + m]).start()

    for m in members:
        pltpu.make_async_copy(lk.at[m], lk_hbm.at[m], out_sem.at[m]).wait()
        pltpu.make_async_copy(ho.at[m], ho_hbm.at[m], out_sem.at[2 + m]).wait()
        for field in range(3):
            for side in range(4):
                edge_copy(field, m, side).wait_send()

        @pl.loop(1, gx)
        def _(k):
            copy1(m, (i + k) % gx).wait_send()

        @pl.loop(1, gy)
        def _(k):
            copy2(m, k).wait_send()

        @pl.when(my_xe != i)
        def _():
            copy3(m, j).wait_send()

        @pl.loop(1, gy)
        def _(k):
            copy3(m, (j + k) % gy).wait_send()


def on_device(gx, gy, white_noise, head_start):
    _, nz, yb, xb = white_noise.shape
    n = yb * gy
    assert n == xb * gx
    zc_n = nz // gx
    rows = zc_n * yb
    wide = yb + 2 * PAD
    matrix = jnp.asarray(split_pair(circulant(n)))
    z_matrix = jnp.asarray(split_pair(np.kron(circulant(nz), np.eye(8))))
    block = jax.ShapeDtypeStruct(white_noise.shape, F32)
    dma = pltpu.SemaphoreType.DMA
    return pl.pallas_call(
        functools.partial(body, gx, gy, n, nz, yb, xb),
        out_shape=(block, block),
        in_specs=[pl.BlockSpec(memory_space=pl.ANY)] * 4,
        out_specs=(pl.BlockSpec(memory_space=pl.ANY),) * 2,
        scratch_shapes=[
            pltpu.VMEM((2, nz, yb, xb), F32),
            pltpu.VMEM((2, n, n), BF16),
            pltpu.VMEM((2, nz * 8, nz * 8), BF16),
            pltpu.VMEM((2, nz, yb, xb), F32),
            pltpu.VMEM((2, gx, zc_n, yb, xb), F32),
            pltpu.VMEM((2 * rows, n), BF16),
            pltpu.VMEM((2, gx, rows, xb), F32),
            pltpu.VMEM((2, gy, yb, xb), F32),
            pltpu.VMEM((n, 2 * xb), BF16),
            pltpu.VMEM((2, gy, yb, xb), F32),
            pltpu.VMEM((2, nz, yb, xb), F32),
            pltpu.VMEM((2, nz, wide, xb), F32),
            pltpu.VMEM((2, nz, wide, xb), F32),
            pltpu.VMEM((2, nz, wide, xb), F32),
            pltpu.VMEM((nz, 6, yb, xb), F32),
            pltpu.VMEM((2, nz, yb, xb), F32),
            pltpu.VMEM((3, 2, 2, nz, xb), F32),
            pltpu.VMEM((3, 2, 2, nz, xb), F32),
            pltpu.VMEM((3, 2, 2, yb, xb), F32),
            pltpu.VMEM((3, 2, 2, yb, xb), F32),
            dma((4,)),
            dma((2,)),
            dma((2,)), dma((2,)),
            dma((2,)), dma((2,)),
            dma((2,)), dma((2,)),
            dma((3, 2, 4)), dma((3, 2, 4)),
            dma((4,)),
        ],
        compiler_params=pltpu.CompilerParams(
            collective_id=0, has_side_effects=True, vmem_limit_bytes=48 * 1024 * 1024
        ),
        cost_estimate=pl.CostEstimate(
            flops=6 * 2 * rows * 2 * n * n, bytes_accessed=16 * n * xb * 4, transcendentals=2 * nz * yb * xb
        ),
    )(white_noise, head_start, matrix, z_matrix)


def solution(mesh):
    spec = P(None, None, "gy", "gx")
    return jax.shard_map(
        functools.partial(on_device, mesh.shape["gx"], mesh.shape["gy"]),
        mesh=mesh,
        in_specs=(spec, spec),
        out_specs=(spec, spec),
        check_vma=False,
    )
```

```python
import functools
import math

import jax
import jax.numpy as jnp
import ml_dtypes
import numpy as np
from jax import lax
from jax.experimental import pallas as pl
from jax.experimental.pallas import tpu as pltpu
from jax.sharding import PartitionSpec as P

F32 = jnp.float32
BF16 = jnp.bfloat16
MESH = pl.DeviceIdType.MESH
PAD = 8


def circulant(length):
    k = np.arange(length)
    q = np.minimum(k, length - k)
    w = 2.0 * math.pi * q / length
    s = 1.0 / (1.0 + (w * (length / 16.0)) ** 2)
    a = np.sqrt(s / np.mean(s))
    taps = np.real(np.fft.ifft(a))
    return taps[(k[:, None] - k[None, :]) % length]


def split_pair(matrix):
    high = matrix.astype(ml_dtypes.bfloat16)
    low = (matrix - high.astype(np.float64)).astype(ml_dtypes.bfloat16)
    return np.stack([high, low])


def split(x):
    high = x.astype(BF16)
    low = (x - high.astype(F32)).astype(BF16)
    return high, low


def dot(a, b):
    return jnp.dot(a, b, preferred_element_type=F32)


def blocks_of(gx, gy, i, j, s):
    if (gx, gy) == (8, 32):
        core, z, y_lo = j % 2, (j // 2) % 8, j // 16
        x, y_hi = i % 4, i // 4
        turn = (x + 2 * core * x) % 4
        return (y_lo + y_hi) % 2 * 16 + (z + turn + 4 * s) % 8 * 2
    return gy // gx * i + 2 * s


def body(
    gx, gy, n, nz, yb, xb,
    w_hbm, h_hbm, c_hbm, kz_hbm, lk_hbm, ho_hbm,
    w_v, c_v, kz_v, zc, r1, bcat, yo, r2, acat, xo, lk,
    hb, rb, gb, wt, ho, row_out, row_in, col_out, col_in,
    in_sem, c_sem, s1, v1, s2, v2, s3, v3, hs, hv, out_sem,
):
    i = lax.axis_index("gx")
    j = lax.axis_index("gy")
    wide = yb + 2 * PAD
    rows = 4 * yb
    members = range(2)

    w_in = [pltpu.make_async_copy(w_hbm.at[m], w_v.at[m], in_sem.at[m]) for m in members]
    h_in = [
        pltpu.make_async_copy(
            h_hbm.at[m], hb.at[m, :, pl.ds(PAD, yb)], in_sem.at[2 + m]
        )
        for m in members
    ]
    kz_in = pltpu.make_async_copy(kz_hbm, kz_v, c_sem.at[0])
    c_in = pltpu.make_async_copy(c_hbm, c_v, c_sem.at[1])
    kz_in.start()
    w_in[0].start()
    w_in[1].start()
    h_in[0].start()
    h_in[1].start()
    c_in.start()

    barrier = pltpu.get_barrier_semaphore()

    @pl.loop(1, gx)
    def _(k):
        pl.semaphore_signal(barrier, inc=1, device_id=((i + k) % gx, j), device_id_type=MESH)

    @pl.loop(1, gy)
    def _(k):
        pl.semaphore_signal(barrier, inc=1, device_id=(i, (j + k) % gy), device_id_type=MESH)

    def filter_z(m):
        for q in range(yb // 8):
            x = w_v[m, :, 8 * q : 8 * q + 8, :].reshape(nz * 8, xb)
            high, low = split(x)
            p = dot(kz_v[0], jnp.concatenate([high, low], axis=1))
            r = p[:, :xb] + p[:, xb:] + dot(kz_v[1], high)
            zc[m, :, 8 * q : 8 * q + 8, :] = r.reshape(nz, 8, xb)
        r1[m, j] = zc[m, j]

    def copy1(m, k):
        peer = (j + k) % gy
        return pltpu.make_async_remote_copy(
            src_ref=zc.at[m, peer],
            dst_ref=r1.at[m, j],
            send_sem=s1.at[m],
            recv_sem=v1.at[m],
            device_id=(i, peer),
            device_id_type=MESH,
        )

    def send1(m):
        @pl.loop(1, gy)
        def _(k):
            copy1(m, k).start()

    kz_in.wait()
    w_in[0].wait()
    filter_z(0)
    pl.semaphore_wait(barrier, gx + gy - 2)
    send1(0)
    w_in[1].wait()
    filter_z(1)
    send1(1)

    lane = lax.broadcasted_iota(jnp.int32, (yb, xb), 1)
    peers = (
        ((i + gx - 1) % gx, j),
        ((i + 1) % gx, j),
        (i, (j + gy - 1) % gy),
        (i, (j + 1) % gy),
    )

    def edge_copy(field, m, side):
        out, inn = (col_out, col_in) if side < 2 else (row_out, row_in)
        return pltpu.make_async_remote_copy(
            src_ref=out.at[field, m, side % 2],
            dst_ref=inn.at[field, m, side % 2],
            send_sem=hs.at[field, m, side],
            recv_sem=hv.at[field, m, side],
            device_id=peers[side],
            device_id_type=MESH,
        )

    def send_edges(field, ref, m):
        for z in range(nz):
            row_out[field, m, 0, z : z + 1, :] = ref[m, z, PAD : PAD + 1, :]
            row_out[field, m, 1, z : z + 1, :] = ref[m, z, PAD + yb - 1 : PAD + yb, :]
        edge_copy(field, m, 2).start()
        edge_copy(field, m, 3).start()

        def pack(z, carry):
            to_left, to_right = carry
            x = ref[m, z, PAD : PAD + yb, :]
            left_at = (2 * z + xb - 1) % xb
            to_left = jnp.where(lane == left_at, pltpu.roll(x, left_at, 1), to_left)
            to_right = jnp.where(lane == 2 * z, pltpu.roll(x, 2 * z + 1, 1), to_right)
            return to_left, to_right

        zero = jnp.zeros((yb, xb), F32)
        to_left, to_right = lax.fori_loop(0, nz, pack, (zero, zero), unroll=4)
        col_out[field, m, 0] = to_left
        col_out[field, m, 1] = to_right
        edge_copy(field, m, 0).start()
        edge_copy(field, m, 1).start()

    def take_edges(field, ref, m):
        for side in range(4):
            edge_copy(field, m, side).wait_recv()
        for z in range(nz):
            ref[m, z, PAD + yb : PAD + yb + 1, :] = row_in[field, m, 0, z : z + 1, :]
            ref[m, z, PAD - 1 : PAD, :] = row_in[field, m, 1, z : z + 1, :]
        return jnp.where(lane % 2 == 0, col_in[field, m, 1], col_in[field, m, 0])

    for m in members:
        h_in[m].wait()
        send_edges(0, hb, m)

    def wait_all(ref, sem):
        pltpu.make_async_copy(ref, ref, sem).wait()

    def copy2(m, to, s):
        return pltpu.make_async_remote_copy(
            src_ref=yo.at[m, pl.ds(blocks_of(gx, gy, to, j, s), 2)],
            dst_ref=r2.at[m, i, s],
            send_sem=s2.at[m],
            recv_sem=v2.at[m],
            device_id=(to, j),
            device_id_type=MESH,
        )

    def filter_y(m):
        per = 256 // yb
        for s in range(gy):
            high, low = split(r1[m, s])
            bcat[s * yb : (s + 1) * yb, 0:xb] = high
            bcat[s * yb : (s + 1) * yb, xb : 2 * xb] = low
        for c in range(n // 256):
            lines = slice(256 * c, 256 * (c + 1))
            p = dot(c_v[0, lines, :], bcat[...])
            r = p[:, :xb] + p[:, xb:] + dot(c_v[1, lines, :], bcat[:, 0:xb])
            yo[m, per * c : per * (c + 1)] = r.reshape(per, yb, xb)
        for s in range(2):
            r2[m, i, s] = yo[m, pl.ds(blocks_of(gx, gy, i, j, s), 2)]

        @pl.loop(1, gx)
        def _(k):
            for s in range(2):
                copy2(m, (i + k) % gx, s).start()

    def copy3(m, to, s, c):
        return pltpu.make_async_remote_copy(
            src_ref=xo.at[m, to, s, c],
            dst_ref=lk.at[m, j],
            send_sem=s3.at[m],
            recv_sem=v3.at[m],
            device_id=(to, blocks_of(gx, gy, i, j, s) + c),
            device_id_type=MESH,
        )

    def each3(m, here, there):
        @pl.loop(0, gx)
        def _(k):
            to = (i + k) % gx
            for s in range(2):
                for c in range(2):
                    own = (to == i) & (blocks_of(gx, gy, i, j, s) + c == j)

                    @pl.when(own)
                    def _():
                        here(m, to, s, c)

                    @pl.when(jnp.logical_not(own))
                    def _():
                        there(m, to, s, c)

    def keep3(m, to, s, c):
        pltpu.make_async_copy(xo.at[m, to, s, c], lk.at[m, j], v3.at[m]).start()

    def filter_x(m):
        for s in range(gx):
            high, low = split(r2[m, s].reshape(rows, xb))
            acat[0:rows, s * xb : (s + 1) * xb] = high
            acat[rows : 2 * rows, s * xb : (s + 1) * xb] = low
        for c in range(n // (2 * xb)):
            cols = slice(2 * xb * c, 2 * xb * (c + 1))
            p = dot(acat[...], c_v[0, :, cols])
            r = p[:rows] + p[rows:] + dot(acat[0:rows, :], c_v[1, :, cols])
            xo[m, 2 * c] = r[:, :xb].reshape(2, 2, yb, xb)
            xo[m, 2 * c + 1] = r[:, xb:].reshape(2, 2, yb, xb)
        each3(m, keep3, lambda *at: copy3(*at).start())

    c_in.wait()
    for m in members:
        wait_all(r1.at[m, pl.ds(0, gy - 1)], v1.at[m])
        filter_y(m)
        wait_all(r2.at[m, pl.ds(0, gx - 1)], v2.at[m])
        filter_x(m)

    row_at = yb * j + lax.broadcasted_iota(jnp.int32, (yb, xb), 0)
    col_at = xb * i + lane
    pinned = (row_at == 0) | (row_at == n - 1) | (col_at == 0) | (col_at == n - 1)

    def sides(ref, m, z, edge):
        x = ref[m, z, PAD : PAD + yb, :]
        e = pltpu.roll(edge, (xb - 2 * z) % xb, 1)
        left = jnp.where(lane == 0, e, pltpu.roll(x, 1, 1))
        right = jnp.where(lane == xb - 1, e, pltpu.roll(x, xb - 1, 1))
        up = ref[m, z, PAD - 1 : PAD - 1 + yb, :]
        down = ref[m, z, PAD + 1 : PAD + 1 + yb, :]
        below = ref[m, z - 1, PAD : PAD + yb, :]
        above = ref[m, z + 1, PAD : PAD + yb, :]
        return x, (left, right, up, down, below, above)

    for m in members:
        wait_all(lk.at[m], v3.at[m])
        pltpu.make_async_copy(lk.at[m], lk_hbm.at[m], out_sem.at[m]).start()

        @pl.loop(0, nz)
        def _(z):
            rb[m, z, PAD : PAD + yb, :] = jnp.exp(-lk[m, z])

        send_edges(1, rb, m)
        h_edge = take_edges(0, hb, m)
        r_edge = take_edges(1, rb, m)

        gb[m, 0, PAD : PAD + yb, :] = hb[m, 0, PAD : PAD + yb, :]
        gb[m, nz - 1, PAD : PAD + yb, :] = hb[m, nz - 1, PAD : PAD + yb, :]
        ho[m, 0] = hb[m, 0, PAD : PAD + yb, :]
        ho[m, nz - 1] = hb[m, nz - 1, PAD : PAD + yb, :]

        @pl.loop(1, nz - 1)
        def _(z):
            r, r_sides = sides(rb, m, z, r_edge)
            h, h_sides = sides(hb, m, z, h_edge)
            weights = [1.0 / (r + r_side) for r_side in r_sides]
            total = sum(weights[1:], weights[0])
            inverse = 1.0 / total
            new = jnp.zeros_like(h)
            for d in range(6):
                weight = weights[d] * inverse
                wt[z, d] = weight
                new = new + weight * h_sides[d]
            gb[m, z, PAD : PAD + yb, :] = jnp.where(pinned, h, new)

        send_edges(2, gb, m)
        g_edge = take_edges(2, gb, m)

        @pl.loop(1, nz - 1)
        def _(z):
            h, h_sides = sides(gb, m, z, g_edge)
            new = jnp.zeros_like(h)
            for d in range(6):
                new = new + wt[z, d] * h_sides[d]
            ho[m, z] = jnp.where(pinned, h, new)

        pltpu.make_async_copy(ho.at[m], ho_hbm.at[m], out_sem.at[2 + m]).start()

    for m in members:
        pltpu.make_async_copy(lk.at[m], lk_hbm.at[m], out_sem.at[m]).wait()
        pltpu.make_async_copy(ho.at[m], ho_hbm.at[m], out_sem.at[2 + m]).wait()
        for field in range(3):
            for side in range(4):
                edge_copy(field, m, side).wait_send()

        @pl.loop(1, gy)
        def _(k):
            copy1(m, k).wait_send()

        @pl.loop(1, gx)
        def _(k):
            for s in range(2):
                copy2(m, (i + k) % gx, s).wait_send()

        each3(m, lambda *at: None, lambda *at: copy3(*at).wait_send())


def on_device(gx, gy, white_noise, head_start):
    _, nz, yb, xb = white_noise.shape
    n = yb * gy
    assert n == xb * gx
    assert n == 4 * yb * gx and nz == gy
    rows = 4 * yb
    wide = yb + 2 * PAD
    matrix = jnp.asarray(split_pair(circulant(n)))
    z_matrix = jnp.asarray(split_pair(np.kron(circulant(nz), np.eye(8))))
    block = jax.ShapeDtypeStruct(white_noise.shape, F32)
    dma = pltpu.SemaphoreType.DMA
    return pl.pallas_call(
        functools.partial(body, gx, gy, n, nz, yb, xb),
        out_shape=(block, block),
        in_specs=[pl.BlockSpec(memory_space=pl.ANY)] * 4,
        out_specs=(pl.BlockSpec(memory_space=pl.ANY),) * 2,
        scratch_shapes=[
            pltpu.VMEM((2, nz, yb, xb), F32),
            pltpu.VMEM((2, n, n), BF16),
            pltpu.VMEM((2, nz * 8, nz * 8), BF16),
            pltpu.VMEM((2, nz, yb, xb), F32),
            pltpu.VMEM((2, gy, yb, xb), F32),
            pltpu.VMEM((n, 2 * xb), BF16),
            pltpu.VMEM((2, gy, yb, xb), F32),
            pltpu.VMEM((2, gx, 2, 2, yb, xb), F32),
            pltpu.VMEM((2 * rows, n), BF16),
            pltpu.VMEM((2, gx, 2, 2, yb, xb), F32),
            pltpu.VMEM((2, nz, yb, xb), F32),
            pltpu.VMEM((2, nz, wide, xb), F32),
            pltpu.VMEM((2, nz, wide, xb), F32),
            pltpu.VMEM((2, nz, wide, xb), F32),
            pltpu.VMEM((nz, 6, yb, xb), F32),
            pltpu.VMEM((2, nz, yb, xb), F32),
            pltpu.VMEM((3, 2, 2, nz, xb), F32),
            pltpu.VMEM((3, 2, 2, nz, xb), F32),
            pltpu.VMEM((3, 2, 2, yb, xb), F32),
            pltpu.VMEM((3, 2, 2, yb, xb), F32),
            dma((4,)),
            dma((2,)),
            dma((2,)), dma((2,)),
            dma((2,)), dma((2,)),
            dma((2,)), dma((2,)),
            dma((3, 2, 4)), dma((3, 2, 4)),
            dma((4,)),
        ],
        compiler_params=pltpu.CompilerParams(
            collective_id=0, has_side_effects=True, vmem_limit_bytes=60 * 1024 * 1024
        ),
        cost_estimate=pl.CostEstimate(
            flops=6 * 2 * rows * 2 * n * n, bytes_accessed=16 * n * xb * 4, transcendentals=2 * nz * yb * xb
        ),
    )(white_noise, head_start, matrix, z_matrix)


def solution(mesh):
    spec = P(None, None, "gy", "gx")
    return jax.shard_map(
        functools.partial(on_device, mesh.shape["gx"], mesh.shape["gy"]),
        mesh=mesh,
        in_specs=(spec, spec),
        out_specs=(spec, spec),
        check_vma=False,
    )
```

```python
import functools
import math

import jax
import jax.numpy as jnp
import ml_dtypes
import numpy as np
from jax import lax
from jax.experimental import pallas as pl
from jax.experimental.pallas import tpu as pltpu
from jax.sharding import PartitionSpec as P

F32 = jnp.float32
BF16 = jnp.bfloat16
MESH = pl.DeviceIdType.MESH
PAD = 8


def circulant(length):
    k = np.arange(length)
    q = np.minimum(k, length - k)
    w = 2.0 * math.pi * q / length
    s = 1.0 / (1.0 + (w * (length / 16.0)) ** 2)
    a = np.sqrt(s / np.mean(s))
    taps = np.real(np.fft.ifft(a))
    return taps[(k[:, None] - k[None, :]) % length]


def split_pair(matrix):
    high = matrix.astype(ml_dtypes.bfloat16)
    low = (matrix - high.astype(np.float64)).astype(ml_dtypes.bfloat16)
    return np.stack([high, low])


def split(x):
    high = x.astype(BF16)
    low = (x - high.astype(F32)).astype(BF16)
    return high, low


def dot(a, b):
    return jnp.dot(a, b, preferred_element_type=F32)


def blocks_of(gx, gy, i, j, s):
    if (gx, gy) == (8, 32):
        core, z, y_lo = j % 2, (j // 2) % 8, j // 16
        x, y_hi = i % 4, i // 4
        turn = (x + 2 * core * x) % 4
        return (y_lo + y_hi) % 2 * 16 + (z + turn + 4 * s) % 8 * 2
    return gy // gx * i + 2 * s


def body(
    gx, gy, n, nz, yb, xb,
    w_hbm, h_hbm, c_hbm, kz_hbm, lk_hbm, ho_hbm,
    w_v, c_v, kz_v, zc, r1, bcat, yo, r2, acat, xo, lk,
    hb, rb, gb, wt, ho, row_out, row_in, col_out, col_in,
    in_sem, c_sem, s1, v1, s2, v2, s3, v3, hs, hv, out_sem,
):
    i = lax.axis_index("gx")
    j = lax.axis_index("gy")
    wide = yb + 2 * PAD
    rows = 4 * yb
    members = range(2)

    w_in = [pltpu.make_async_copy(w_hbm.at[m], w_v.at[m], in_sem.at[m]) for m in members]
    h_in = [
        pltpu.make_async_copy(
            h_hbm.at[m], hb.at[m, :, pl.ds(PAD, yb)], in_sem.at[2 + m]
        )
        for m in members
    ]
    kz_in = pltpu.make_async_copy(kz_hbm, kz_v, c_sem.at[0])
    c_in = pltpu.make_async_copy(c_hbm, c_v, c_sem.at[1])
    kz_in.start()
    w_in[0].start()
    w_in[1].start()
    h_in[0].start()
    h_in[1].start()
    c_in.start()

    barrier = pltpu.get_barrier_semaphore()

    @pl.loop(1, gx)
    def _(k):
        pl.semaphore_signal(barrier, inc=1, device_id=((i + k) % gx, j), device_id_type=MESH)

    @pl.loop(1, gy)
    def _(k):
        pl.semaphore_signal(barrier, inc=1, device_id=(i, (j + k) % gy), device_id_type=MESH)

    def filter_z(m):
        for q in range(yb // 8):
            x = w_v[m, :, 8 * q : 8 * q + 8, :].reshape(nz * 8, xb)
            high, low = split(x)
            p = dot(kz_v[0], jnp.concatenate([high, low], axis=1))
            r = p[:, :xb] + p[:, xb:] + dot(kz_v[1], high)
            zc[m, :, 8 * q : 8 * q + 8, :] = r.reshape(nz, 8, xb)
        r1[m, j] = zc[m, j]

    def copy1(m, k):
        peer = (j + k) % gy
        return pltpu.make_async_remote_copy(
            src_ref=zc.at[m, peer],
            dst_ref=r1.at[m, j],
            send_sem=s1.at[m],
            recv_sem=v1.at[m],
            device_id=(i, peer),
            device_id_type=MESH,
        )

    def send1(m):
        @pl.loop(1, gy)
        def _(k):
            copy1(m, k).start()

    kz_in.wait()
    w_in[0].wait()
    filter_z(0)
    pl.semaphore_wait(barrier, gx + gy - 2)
    send1(0)
    w_in[1].wait()
    filter_z(1)
    send1(1)

    lane = lax.broadcasted_iota(jnp.int32, (yb, xb), 1)
    first, last = lane == 0, lane == xb - 1
    even = lane % 2 == 0
    peers = (
        ((i + gx - 1) % gx, j),
        ((i + 1) % gx, j),
        (i, (j + gy - 1) % gy),
        (i, (j + 1) % gy),
    )

    def edge_copy(field, m, side):
        out, inn = (col_out, col_in) if side < 2 else (row_out, row_in)
        return pltpu.make_async_remote_copy(
            src_ref=out.at[field, m, side % 2],
            dst_ref=inn.at[field, m, side % 2],
            send_sem=hs.at[field, m, side],
            recv_sem=hv.at[field, m, side],
            device_id=peers[side],
            device_id_type=MESH,
        )

    zero = jnp.zeros((yb, xb), F32)

    def pack(field, m, z, x, packed):
        to_left, to_right = packed
        row_out[field, m, 0, pl.ds(z, 1), :] = x[0:1]
        row_out[field, m, 1, pl.ds(z, 1), :] = x[yb - 1 : yb]
        left_at = (2 * z + xb - 1) % xb
        to_left = jnp.where(lane == left_at, pltpu.roll(x, left_at, 1), to_left)
        to_right = jnp.where(lane == 2 * z, pltpu.roll(x, 2 * z + 1, 1), to_right)
        return to_left, to_right

    def send_edges(field, m, packed):
        col_out[field, m, 0] = packed[0]
        col_out[field, m, 1] = packed[1]
        for side in range(4):
            edge_copy(field, m, side).start()

    def take_edges(field, ref, m):
        for side in range(4):
            edge_copy(field, m, side).wait_recv()
        for z in range(nz):
            ref[m, z, PAD + yb : PAD + yb + 1, :] = row_in[field, m, 0, z : z + 1, :]
            ref[m, z, PAD - 1 : PAD, :] = row_in[field, m, 1, z : z + 1, :]
        return jnp.where(even, col_in[field, m, 1], col_in[field, m, 0])

    def own_edges(field, m):
        left = pltpu.roll(col_out[field, m, 0], 1, 1)
        right = pltpu.roll(col_out[field, m, 1], xb - 1, 1)
        return jnp.where(even, left, right)

    for m in members:
        h_in[m].wait()

        def pack_head(z, packed):
            return pack(0, m, z, hb[m, z, PAD : PAD + yb, :], packed)

        send_edges(0, m, lax.fori_loop(0, nz, pack_head, (zero, zero), unroll=16))

    def wait_all(ref, sem):
        pltpu.make_async_copy(ref, ref, sem).wait()

    def copy2(m, to, s):
        return pltpu.make_async_remote_copy(
            src_ref=yo.at[m, pl.ds(blocks_of(gx, gy, to, j, s), 2)],
            dst_ref=r2.at[m, i, s],
            send_sem=s2.at[m],
            recv_sem=v2.at[m],
            device_id=(to, j),
            device_id_type=MESH,
        )

    def filter_y(m):
        per = 256 // yb
        for s in range(gy):
            high, low = split(r1[m, s])
            bcat[s * yb : (s + 1) * yb, 0:xb] = high
            bcat[s * yb : (s + 1) * yb, xb : 2 * xb] = low
        for c in range(n // 256):
            lines = slice(256 * c, 256 * (c + 1))
            p = dot(c_v[0, lines, :], bcat[...])
            r = p[:, :xb] + p[:, xb:] + dot(c_v[1, lines, :], bcat[:, 0:xb])
            yo[m, per * c : per * (c + 1)] = r.reshape(per, yb, xb)
        for s in range(2):
            r2[m, i, s] = yo[m, pl.ds(blocks_of(gx, gy, i, j, s), 2)]

        @pl.loop(1, gx)
        def _(k):
            for s in range(2):
                copy2(m, (i + k) % gx, s).start()

    def copy3(m, to, s, c):
        return pltpu.make_async_remote_copy(
            src_ref=xo.at[m, to, s, c],
            dst_ref=lk.at[m, j],
            send_sem=s3.at[m],
            recv_sem=v3.at[m],
            device_id=(to, blocks_of(gx, gy, i, j, s) + c),
            device_id_type=MESH,
        )

    def each3(m, here, there):
        @pl.loop(0, gx)
        def _(k):
            to = (i + k) % gx
            for s in range(2):
                for c in range(2):
                    own = (to == i) & (blocks_of(gx, gy, i, j, s) + c == j)

                    @pl.when(own)
                    def _():
                        here(m, to, s, c)

                    @pl.when(jnp.logical_not(own))
                    def _():
                        there(m, to, s, c)

    def keep3(m, to, s, c):
        pltpu.make_async_copy(xo.at[m, to, s, c], lk.at[m, j], v3.at[m]).start()

    def filter_x(m):
        for s in range(gx):
            high, low = split(r2[m, s].reshape(rows, xb))
            acat[0:rows, s * xb : (s + 1) * xb] = high
            acat[rows : 2 * rows, s * xb : (s + 1) * xb] = low
        for c in range(n // (2 * xb)):
            cols = slice(2 * xb * c, 2 * xb * (c + 1))
            p = dot(acat[...], c_v[0, :, cols])
            r = p[:rows] + p[rows:] + dot(acat[0:rows, :], c_v[1, :, cols])
            xo[m, 2 * c] = r[:, :xb].reshape(2, 2, yb, xb)
            xo[m, 2 * c + 1] = r[:, xb:].reshape(2, 2, yb, xb)
        each3(m, keep3, lambda *at: copy3(*at).start())

    c_in.wait()
    for m in members:
        wait_all(r1.at[m, pl.ds(0, gy - 1)], v1.at[m])
        filter_y(m)
        wait_all(r2.at[m, pl.ds(0, gx - 1)], v2.at[m])
        filter_x(m)

    row_at = yb * j + lax.broadcasted_iota(jnp.int32, (yb, xb), 0)
    col_at = xb * i + lane
    pinned = (row_at == 0) | (row_at == n - 1) | (col_at == 0) | (col_at == n - 1)

    def inverse(x):
        guess = pl.reciprocal(x, approx=True)
        return guess * (2.0 - x * guess)

    def layer(ref, m, z):
        return ref[m, z, PAD : PAD + yb, :]

    def above(ref, m, z):
        return ref[m, z, PAD - 1 : PAD - 1 + yb, :]

    def under(ref, m, z):
        return ref[m, z, PAD + 1 : PAD + 1 + yb, :]

    def to_lane(packed, z):
        return pltpu.roll(packed, (xb - 2 * z) % xb, 1)

    def flow_x(w, h, edge_w, edge_h, z):
        right = jnp.where(last, to_lane(edge_w, z), w)
        w_left = jnp.where(first, to_lane(edge_w, z), pltpu.roll(w, 1, 1))
        e = to_lane(edge_h, z)
        h_right = jnp.where(last, e, pltpu.roll(h, xb - 1, 1))
        h_left = jnp.where(first, e, pltpu.roll(h, 1, 1))
        return right * h_right + w_left * h_left, right + w_left

    for m in members:
        wait_all(lk.at[m], v3.at[m])
        pltpu.make_async_copy(lk.at[m], lk_hbm.at[m], out_sem.at[m]).start()

        def resist(z, packed):
            r = jnp.exp(-lk[m, z])
            rb[m, z, PAD : PAD + yb, :] = r
            return pack(1, m, z, r, packed)

        send_edges(1, m, lax.fori_loop(0, nz, resist, (zero, zero), unroll=True))
        h_edge = take_edges(0, hb, m)
        r_edge = take_edges(1, rb, m)
        w_edge = inverse(own_edges(1, m) + r_edge)

        for z in (0, nz - 1):
            gb[m, z, PAD : PAD + yb, :] = layer(hb, m, z)
            ho[m, z] = layer(hb, m, z)

        def sweep(z, carry):
            r, h_low, h, w_low, packed = carry
            r_high = layer(rb, m, z + 1)
            h_high = layer(hb, m, z + 1)
            w_high = inverse(r + r_high)
            w_up = inverse(r + above(rb, m, z))
            w_down = inverse(r + under(rb, m, z))
            w_x = inverse(r + pltpu.roll(r, xb - 1, 1))
            gain, total = flow_x(w_x, h, w_edge, h_edge, z)
            total = total + ((w_low + w_high) + (w_up + w_down))
            gain = gain + (w_low * h_low + w_high * h_high)
            gain = gain + (w_up * above(hb, m, z) + w_down * under(hb, m, z))
            share = inverse(total)
            new = jnp.where(pinned, h, gain * share)
            gb[m, z, PAD : PAD + yb, :] = new
            wt[0, z] = w_x
            wt[1, z] = w_high
            wt[2, z] = w_up
            wt[3, z] = w_down
            wt[4, z] = share
            return r_high, h, h_high, w_high, pack(2, m, z, new, packed)

        r0, r1_ = layer(rb, m, 0), layer(rb, m, 1)
        w_first = inverse(r0 + r1_)
        start = (r1_, layer(hb, m, 0), layer(hb, m, 1), w_first, (zero, zero))
        packed = lax.fori_loop(1, nz - 1, sweep, start, unroll=6)[-1]
        send_edges(2, m, packed)
        g_edge = take_edges(2, gb, m)

        def again(z, carry):
            h_low, h, w_low = carry
            h_high = layer(gb, m, z + 1)
            w_high = wt[1, z]
            gain, _ = flow_x(wt[0, z], h, w_edge, g_edge, z)
            gain = gain + (w_low * h_low + w_high * h_high)
            gain = gain + (wt[2, z] * above(gb, m, z) + wt[3, z] * under(gb, m, z))
            ho[m, z] = jnp.where(pinned, h, gain * wt[4, z])
            return h, h_high, w_high

        again_start = (layer(gb, m, 0), layer(gb, m, 1), w_first)
        lax.fori_loop(1, nz - 1, again, again_start, unroll=10)
        pltpu.make_async_copy(ho.at[m], ho_hbm.at[m], out_sem.at[2 + m]).start()

    for m in members:
        pltpu.make_async_copy(lk.at[m], lk_hbm.at[m], out_sem.at[m]).wait()
        pltpu.make_async_copy(ho.at[m], ho_hbm.at[m], out_sem.at[2 + m]).wait()
        for field in range(3):
            for side in range(4):
                edge_copy(field, m, side).wait_send()

        @pl.loop(1, gy)
        def _(k):
            copy1(m, k).wait_send()

        @pl.loop(1, gx)
        def _(k):
            for s in range(2):
                copy2(m, (i + k) % gx, s).wait_send()

        each3(m, lambda *at: None, lambda *at: copy3(*at).wait_send())


def on_device(gx, gy, white_noise, head_start):
    _, nz, yb, xb = white_noise.shape
    n = yb * gy
    assert n == xb * gx
    assert n == 4 * yb * gx and nz == gy
    rows = 4 * yb
    wide = yb + 2 * PAD
    matrix = jnp.asarray(split_pair(circulant(n)))
    z_matrix = jnp.asarray(split_pair(np.kron(circulant(nz), np.eye(8))))
    block = jax.ShapeDtypeStruct(white_noise.shape, F32)
    dma = pltpu.SemaphoreType.DMA
    return pl.pallas_call(
        functools.partial(body, gx, gy, n, nz, yb, xb),
        out_shape=(block, block),
        in_specs=[pl.BlockSpec(memory_space=pl.ANY)] * 4,
        out_specs=(pl.BlockSpec(memory_space=pl.ANY),) * 2,
        scratch_shapes=[
            pltpu.VMEM((2, nz, yb, xb), F32),
            pltpu.VMEM((2, n, n), BF16),
            pltpu.VMEM((2, nz * 8, nz * 8), BF16),
            pltpu.VMEM((2, nz, yb, xb), F32),
            pltpu.VMEM((2, gy, yb, xb), F32),
            pltpu.VMEM((n, 2 * xb), BF16),
            pltpu.VMEM((2, gy, yb, xb), F32),
            pltpu.VMEM((2, gx, 2, 2, yb, xb), F32),
            pltpu.VMEM((2 * rows, n), BF16),
            pltpu.VMEM((2, gx, 2, 2, yb, xb), F32),
            pltpu.VMEM((2, nz, yb, xb), F32),
            pltpu.VMEM((2, nz, wide, xb), F32),
            pltpu.VMEM((2, nz, wide, xb), F32),
            pltpu.VMEM((2, nz, wide, xb), F32),
            pltpu.VMEM((5, nz, yb, xb), F32),
            pltpu.VMEM((2, nz, yb, xb), F32),
            pltpu.VMEM((3, 2, 2, nz, xb), F32),
            pltpu.VMEM((3, 2, 2, nz, xb), F32),
            pltpu.VMEM((3, 2, 2, yb, xb), F32),
            pltpu.VMEM((3, 2, 2, yb, xb), F32),
            dma((4,)),
            dma((2,)),
            dma((2,)), dma((2,)),
            dma((2,)), dma((2,)),
            dma((2,)), dma((2,)),
            dma((3, 2, 4)), dma((3, 2, 4)),
            dma((4,)),
        ],
        compiler_params=pltpu.CompilerParams(
            collective_id=0, has_side_effects=True, vmem_limit_bytes=60 * 1024 * 1024
        ),
        cost_estimate=pl.CostEstimate(
            flops=6 * 2 * rows * 2 * n * n, bytes_accessed=16 * n * xb * 4, transcendentals=2 * nz * yb * xb
        ),
    )(white_noise, head_start, matrix, z_matrix)


def solution(mesh):
    spec = P(None, None, "gy", "gx")
    return jax.shard_map(
        functools.partial(on_device, mesh.shape["gx"], mesh.shape["gy"]),
        mesh=mesh,
        in_specs=(spec, spec),
        out_specs=(spec, spec),
        check_vma=False,
    )
```

```python
import functools
import math

import jax
import jax.numpy as jnp
import ml_dtypes
import numpy as np
from jax import lax
from jax.experimental import pallas as pl
from jax.experimental.pallas import tpu as pltpu
from jax.sharding import PartitionSpec as P

F32 = jnp.float32
BF16 = jnp.bfloat16
MESH = pl.DeviceIdType.MESH
PAD = 8


def circulant(length):
    k = np.arange(length)
    q = np.minimum(k, length - k)
    w = 2.0 * math.pi * q / length
    s = 1.0 / (1.0 + (w * (length / 16.0)) ** 2)
    a = np.sqrt(s / np.mean(s))
    taps = np.real(np.fft.ifft(a))
    return taps[(k[:, None] - k[None, :]) % length]


def split_pair(matrix):
    high = matrix.astype(ml_dtypes.bfloat16)
    low = (matrix - high.astype(np.float64)).astype(ml_dtypes.bfloat16)
    return np.stack([high, low])


def split(x):
    high = x.astype(BF16)
    low = (x - high.astype(F32)).astype(BF16)
    return high, low


def dot(a, b):
    return jnp.dot(a, b, preferred_element_type=F32)


def blocks_of(gx, gy, i, j, s):
    if (gx, gy) == (8, 32):
        core, z, y_lo = j % 2, (j // 2) % 8, j // 16
        x, y_hi = i % 4, i // 4
        turn = (x + 2 * core * x) % 4
        return (y_lo + y_hi) % 2 * 16 + (z + turn + 4 * s) % 8 * 2
    return gy // gx * i + 2 * s


def body(
    gx, gy, n, nz, yb, xb,
    w_hbm, h_hbm, c_hbm, kz_hbm, lk_hbm, ho_hbm,
    w_v, c_v, kz_v, zc, r1, bcat, yo, r2, acat, xo, lk,
    hb, rb, gb, wt, ho, row_out, row_in, col_out, col_in,
    in_sem, c_sem, s1, v1, s2, v2, s3, v3, hs, hv, out_sem,
):
    i = lax.axis_index("gx")
    j = lax.axis_index("gy")
    wide = yb + 2 * PAD
    rows = 4 * yb
    members = range(2)

    w_in = [pltpu.make_async_copy(w_hbm.at[m], w_v.at[m], in_sem.at[m]) for m in members]
    h_in = [
        pltpu.make_async_copy(
            h_hbm.at[m], hb.at[m, :, pl.ds(PAD, yb)], in_sem.at[2 + m]
        )
        for m in members
    ]
    kz_in = pltpu.make_async_copy(kz_hbm, kz_v, c_sem.at[0])
    c_in = pltpu.make_async_copy(c_hbm, c_v, c_sem.at[1])
    kz_in.start()
    w_in[0].start()
    w_in[1].start()
    h_in[0].start()
    h_in[1].start()
    c_in.start()

    barrier = pltpu.get_barrier_semaphore()

    @pl.loop(1, gx)
    def _(k):
        pl.semaphore_signal(barrier, inc=1, device_id=((i + k) % gx, j), device_id_type=MESH)

    @pl.loop(1, gy)
    def _(k):
        pl.semaphore_signal(barrier, inc=1, device_id=(i, (j + k) % gy), device_id_type=MESH)

    def filter_z(m):
        for q in range(yb // 8):
            x = w_v[m, :, 8 * q : 8 * q + 8, :].reshape(nz * 8, xb)
            high, low = split(x)
            p = dot(kz_v[0], jnp.concatenate([high, low], axis=1))
            r = p[:, :xb] + p[:, xb:] + dot(kz_v[1], high)
            zc[m, :, 8 * q : 8 * q + 8, :] = r.reshape(nz, 8, xb)
        r1[m, j] = zc[m, j]

    def copy1(m, k):
        peer = (j + k) % gy
        return pltpu.make_async_remote_copy(
            src_ref=zc.at[m, peer],
            dst_ref=r1.at[m, j],
            send_sem=s1.at[m],
            recv_sem=v1.at[m],
            device_id=(i, peer),
            device_id_type=MESH,
        )

    def send1(m):
        @pl.loop(1, gy)
        def _(k):
            copy1(m, k).start()

    kz_in.wait()
    w_in[0].wait()
    filter_z(0)
    pl.semaphore_wait(barrier, gx + gy - 2)
    send1(0)
    w_in[1].wait()
    filter_z(1)
    send1(1)

    lane = lax.broadcasted_iota(jnp.int32, (yb, xb), 1)
    first, last = lane == 0, lane == xb - 1
    even = lane % 2 == 0
    peers = (
        ((i + gx - 1) % gx, j),
        ((i + 1) % gx, j),
        (i, (j + gy - 1) % gy),
        (i, (j + 1) % gy),
    )

    def edge_copy(field, m, side):
        out, inn = (col_out, col_in) if side < 2 else (row_out, row_in)
        return pltpu.make_async_remote_copy(
            src_ref=out.at[field, m, side % 2],
            dst_ref=inn.at[field, m, side % 2],
            send_sem=hs.at[field, m, side],
            recv_sem=hv.at[field, m, side],
            device_id=peers[side],
            device_id_type=MESH,
        )

    zero = jnp.zeros((yb, xb), F32)

    def pack(field, m, z, x, packed):
        to_left, to_right = packed
        row_out[field, m, 0, pl.ds(z, 1), :] = x[0:1]
        row_out[field, m, 1, pl.ds(z, 1), :] = x[yb - 1 : yb]
        left_at = (2 * z + xb - 1) % xb
        to_left = jnp.where(lane == left_at, pltpu.roll(x, left_at, 1), to_left)
        to_right = jnp.where(lane == 2 * z, pltpu.roll(x, 2 * z + 1, 1), to_right)
        return to_left, to_right

    def send_edges(field, m, packed):
        col_out[field, m, 0] = packed[0]
        col_out[field, m, 1] = packed[1]
        for side in range(4):
            edge_copy(field, m, side).start()

    def take_edges(field, ref, m):
        for side in range(4):
            edge_copy(field, m, side).wait_recv()
        for z in range(nz):
            ref[m, z, PAD + yb : PAD + yb + 1, :] = row_in[field, m, 0, z : z + 1, :]
            ref[m, z, PAD - 1 : PAD, :] = row_in[field, m, 1, z : z + 1, :]
        return jnp.where(even, col_in[field, m, 1], col_in[field, m, 0])

    def own_edges(field, m):
        left = pltpu.roll(col_out[field, m, 0], 1, 1)
        right = pltpu.roll(col_out[field, m, 1], xb - 1, 1)
        return jnp.where(even, left, right)

    for m in members:
        h_in[m].wait()

        def pack_head(z, packed):
            return pack(0, m, z, hb[m, z, PAD : PAD + yb, :], packed)

        send_edges(0, m, lax.fori_loop(0, nz, pack_head, (zero, zero), unroll=16))

    def wait_all(ref, sem):
        pltpu.make_async_copy(ref, ref, sem).wait()

    def copy2(m, to, s):
        return pltpu.make_async_remote_copy(
            src_ref=yo.at[m, pl.ds(blocks_of(gx, gy, to, j, s), 2)],
            dst_ref=r2.at[m, i, s],
            send_sem=s2.at[m],
            recv_sem=v2.at[m],
            device_id=(to, j),
            device_id_type=MESH,
        )

    def filter_y(m):
        per = 256 // yb
        for s in range(gy):
            high, low = split(r1[m, s])
            bcat[s * yb : (s + 1) * yb, 0:xb] = high
            bcat[s * yb : (s + 1) * yb, xb : 2 * xb] = low
        for c in range(n // 256):
            lines = slice(256 * c, 256 * (c + 1))
            p = dot(c_v[0, lines, :], bcat[...])
            r = p[:, :xb] + p[:, xb:] + dot(c_v[1, lines, :], bcat[:, 0:xb])
            yo[m, per * c : per * (c + 1)] = r.reshape(per, yb, xb)
        for s in range(2):
            r2[m, i, s] = yo[m, pl.ds(blocks_of(gx, gy, i, j, s), 2)]

        @pl.loop(1, gx)
        def _(k):
            for s in range(2):
                copy2(m, (i + k) % gx, s).start()

    def copy3(m, to, s, c):
        return pltpu.make_async_remote_copy(
            src_ref=xo.at[m, to, s, c],
            dst_ref=lk.at[m, j],
            send_sem=s3.at[m],
            recv_sem=v3.at[m],
            device_id=(to, blocks_of(gx, gy, i, j, s) + c),
            device_id_type=MESH,
        )

    def each3(m, here, there):
        @pl.loop(0, gx)
        def _(k):
            to = (i + k) % gx
            for s in range(2):
                for c in range(2):
                    own = (to == i) & (blocks_of(gx, gy, i, j, s) + c == j)

                    @pl.when(own)
                    def _():
                        here(m, to, s, c)

                    @pl.when(jnp.logical_not(own))
                    def _():
                        there(m, to, s, c)

    def keep3(m, to, s, c):
        pltpu.make_async_copy(xo.at[m, to, s, c], lk.at[m, j], v3.at[m]).start()

    def filter_x(m):
        for s in range(gx):
            high, low = split(r2[m, s].reshape(rows, xb))
            acat[0:rows, s * xb : (s + 1) * xb] = high
            acat[rows : 2 * rows, s * xb : (s + 1) * xb] = low
        for c in range(n // (2 * xb)):
            cols = slice(2 * xb * c, 2 * xb * (c + 1))
            p = dot(acat[...], c_v[0, :, cols])
            r = p[:rows] + p[rows:] + dot(acat[0:rows, :], c_v[1, :, cols])
            xo[m, 2 * c] = r[:, :xb].reshape(2, 2, yb, xb)
            xo[m, 2 * c + 1] = r[:, xb:].reshape(2, 2, yb, xb)
        each3(m, keep3, lambda *at: copy3(*at).start())

    c_in.wait()
    for m in members:
        wait_all(r1.at[m, pl.ds(0, gy - 1)], v1.at[m])
        filter_y(m)
        wait_all(r2.at[m, pl.ds(0, gx - 1)], v2.at[m])
        filter_x(m)

    row_at = yb * j + lax.broadcasted_iota(jnp.int32, (yb, xb), 0)
    col_at = xb * i + lane
    pinned = (row_at == 0) | (row_at == n - 1) | (col_at == 0) | (col_at == n - 1)

    def inverse(x):
        guess = pl.reciprocal(x, approx=True)
        return guess * (2.0 - x * guess)

    def layer(ref, m, z):
        return ref[m, z, PAD : PAD + yb, :]

    def above(ref, m, z):
        return ref[m, z, PAD - 1 : PAD - 1 + yb, :]

    def under(ref, m, z):
        return ref[m, z, PAD + 1 : PAD + 1 + yb, :]

    def to_lane(packed, z):
        return pltpu.roll(packed, (xb - 2 * z) % xb, 1)

    def flow_x(w, h, edge_w, edge_h, z):
        right = jnp.where(last, to_lane(edge_w, z), w)
        w_left = jnp.where(first, to_lane(edge_w, z), pltpu.roll(w, 1, 1))
        e = to_lane(edge_h, z)
        h_right = jnp.where(last, e, pltpu.roll(h, xb - 1, 1))
        h_left = jnp.where(first, e, pltpu.roll(h, 1, 1))
        return right * h_right + w_left * h_left, right + w_left

    def resist(m):
        wait_all(lk.at[m], v3.at[m])
        pltpu.make_async_copy(lk.at[m], lk_hbm.at[m], out_sem.at[m]).start()

        def step(z, packed):
            r = jnp.exp(-lk[m, z])
            rb[m, z, PAD : PAD + yb, :] = r
            return pack(1, m, z, r, packed)

        send_edges(1, m, lax.fori_loop(0, nz, step, (zero, zero), unroll=True))
        for z in (0, nz - 1):
            gb[m, z, PAD : PAD + yb, :] = layer(hb, m, z)
            ho[m, z] = layer(hb, m, z)

    def first_sweep(m):
        h_edge = take_edges(0, hb, m)
        r_edge = take_edges(1, rb, m)
        w_edge = inverse(own_edges(1, m) + r_edge)

        def step(z, carry):
            r, h_low, h, w_low, packed = carry
            r_high = layer(rb, m, z + 1)
            h_high = layer(hb, m, z + 1)
            w_high = inverse(r + r_high)
            w_up = inverse(r + above(rb, m, z))
            w_down = inverse(r + under(rb, m, z))
            w_x = inverse(r + pltpu.roll(r, xb - 1, 1))
            gain, total = flow_x(w_x, h, w_edge, h_edge, z)
            total = total + ((w_low + w_high) + (w_up + w_down))
            gain = gain + (w_low * h_low + w_high * h_high)
            gain = gain + (w_up * above(hb, m, z) + w_down * under(hb, m, z))
            share = inverse(total)
            new = jnp.where(pinned, h, gain * share)
            gb[m, z, PAD : PAD + yb, :] = new
            wt[m, 0, z] = w_x
            wt[m, 1, z] = w_high
            wt[m, 2, z] = w_up
            wt[m, 3, z] = w_down
            wt[m, 4, z] = share
            return r_high, h, h_high, w_high, pack(2, m, z, new, packed)

        r0, r1_ = layer(rb, m, 0), layer(rb, m, 1)
        w_first = inverse(r0 + r1_)
        wt[m, 1, 0] = w_first
        start = (r1_, layer(hb, m, 0), layer(hb, m, 1), w_first, (zero, zero))
        send_edges(2, m, lax.fori_loop(1, nz - 1, step, start, unroll=6)[-1])
        return w_edge

    def second_sweep(m, w_edge):
        g_edge = take_edges(2, gb, m)

        def step(z, carry):
            h_low, h, w_low = carry
            h_high = layer(gb, m, z + 1)
            w_high = wt[m, 1, z]
            gain, _ = flow_x(wt[m, 0, z], h, w_edge, g_edge, z)
            gain = gain + (w_low * h_low + w_high * h_high)
            gain = gain + (wt[m, 2, z] * above(gb, m, z) + wt[m, 3, z] * under(gb, m, z))
            ho[m, z] = jnp.where(pinned, h, gain * wt[m, 4, z])
            return h, h_high, w_high

        start = (layer(gb, m, 0), layer(gb, m, 1), wt[m, 1, 0])
        lax.fori_loop(1, nz - 1, step, start, unroll=10)
        pltpu.make_async_copy(ho.at[m], ho_hbm.at[m], out_sem.at[2 + m]).start()

    for m in members:
        resist(m)
    w_edges = [first_sweep(m) for m in members]
    for m in members:
        second_sweep(m, w_edges[m])

    for m in members:
        pltpu.make_async_copy(lk.at[m], lk_hbm.at[m], out_sem.at[m]).wait()
        pltpu.make_async_copy(ho.at[m], ho_hbm.at[m], out_sem.at[2 + m]).wait()
        for field in range(3):
            for side in range(4):
                edge_copy(field, m, side).wait_send()

        @pl.loop(1, gy)
        def _(k):
            copy1(m, k).wait_send()

        @pl.loop(1, gx)
        def _(k):
            for s in range(2):
                copy2(m, (i + k) % gx, s).wait_send()

        each3(m, lambda *at: None, lambda *at: copy3(*at).wait_send())


def hand_over(lk_ref, ho_ref, lk_out, ho_out, sem):
    copies = [
        pltpu.make_async_copy(source.at[m], target.at[m], sem.at[2 * at + m])
        for at, (source, target) in enumerate(((lk_ref, lk_out), (ho_ref, ho_out)))
        for m in range(2)
    ]
    for copy in copies:
        copy.start()
    for copy in copies:
        copy.wait()


def on_device(gx, gy, white_noise, head_start):
    _, nz, yb, xb = white_noise.shape
    n = yb * gy
    assert n == xb * gx
    assert n == 4 * yb * gx and nz == gy
    rows = 4 * yb
    wide = yb + 2 * PAD
    matrix = jnp.asarray(split_pair(circulant(n)))
    z_matrix = jnp.asarray(split_pair(np.kron(circulant(nz), np.eye(8))))
    block = jax.ShapeDtypeStruct(white_noise.shape, F32)
    dma = pltpu.SemaphoreType.DMA
    results = pl.pallas_call(
        functools.partial(body, gx, gy, n, nz, yb, xb),
        out_shape=(pltpu.VMEM(block.shape, F32),) * 2,
        in_specs=[pl.BlockSpec(memory_space=pl.ANY)] * 4,
        out_specs=(pl.BlockSpec(memory_space=pl.ANY),) * 2,
        scratch_shapes=[
            pltpu.VMEM((2, nz, yb, xb), F32),
            pltpu.VMEM((2, n, n), BF16),
            pltpu.VMEM((2, nz * 8, nz * 8), BF16),
            pltpu.VMEM((2, nz, yb, xb), F32),
            pltpu.VMEM((2, gy, yb, xb), F32),
            pltpu.VMEM((n, 2 * xb), BF16),
            pltpu.VMEM((2, gy, yb, xb), F32),
            pltpu.VMEM((2, gx, 2, 2, yb, xb), F32),
            pltpu.VMEM((2 * rows, n), BF16),
            pltpu.VMEM((2, gx, 2, 2, yb, xb), F32),
            pltpu.VMEM((2, nz, yb, xb), F32),
            pltpu.VMEM((2, nz, wide, xb), F32),
            pltpu.VMEM((2, nz, wide, xb), F32),
            pltpu.VMEM((2, nz, wide, xb), F32),
            pltpu.VMEM((2, 5, nz, yb, xb), F32),
            pltpu.VMEM((2, nz, yb, xb), F32),
            pltpu.VMEM((3, 2, 2, nz, xb), F32),
            pltpu.VMEM((3, 2, 2, nz, xb), F32),
            pltpu.VMEM((3, 2, 2, yb, xb), F32),
            pltpu.VMEM((3, 2, 2, yb, xb), F32),
            dma((4,)),
            dma((2,)),
            dma((2,)), dma((2,)),
            dma((2,)), dma((2,)),
            dma((2,)), dma((2,)),
            dma((3, 2, 4)), dma((3, 2, 4)),
            dma((4,)),
        ],
        compiler_params=pltpu.CompilerParams(
            collective_id=0, has_side_effects=True, vmem_limit_bytes=60 * 1024 * 1024
        ),
        cost_estimate=pl.CostEstimate(
            flops=6 * 2 * rows * 2 * n * n, bytes_accessed=16 * n * xb * 4, transcendentals=2 * nz * yb * xb
        ),
    )(white_noise, head_start, matrix, z_matrix)
    return pl.pallas_call(
        hand_over,
        out_shape=(block, block),
        in_specs=[pl.BlockSpec(memory_space=pl.ANY)] * 2,
        out_specs=(pl.BlockSpec(memory_space=pl.ANY),) * 2,
        scratch_shapes=[dma((4,))],
    )(*results)


def solution(mesh):
    spec = P(None, None, "gy", "gx")
    return jax.shard_map(
        functools.partial(on_device, mesh.shape["gx"], mesh.shape["gy"]),
        mesh=mesh,
        in_specs=(spec, spec),
        out_specs=(spec, spec),
        check_vma=False,
    )
```

```python
import functools
import math

import jax
import jax.numpy as jnp
import ml_dtypes
import numpy as np
from jax import lax
from jax.experimental import pallas as pl
from jax.experimental.pallas import tpu as pltpu
from jax.sharding import PartitionSpec as P

F32 = jnp.float32
BF16 = jnp.bfloat16
MESH = pl.DeviceIdType.MESH
PAD = 8


def circulant(length):
    k = np.arange(length)
    q = np.minimum(k, length - k)
    w = 2.0 * math.pi * q / length
    s = 1.0 / (1.0 + (w * (length / 16.0)) ** 2)
    a = np.sqrt(s / np.mean(s))
    taps = np.real(np.fft.ifft(a))
    return taps[(k[:, None] - k[None, :]) % length]


def split_pair(matrix):
    high = matrix.astype(ml_dtypes.bfloat16)
    low = (matrix - high.astype(np.float64)).astype(ml_dtypes.bfloat16)
    return np.stack([high, low])


def split(x):
    high = x.astype(BF16)
    low = (x - high.astype(F32)).astype(BF16)
    return high, low


def dot(a, b):
    return jnp.dot(a, b, preferred_element_type=F32)


def blocks_of(gx, gy, i, j, half):
    if (gx, gy) == (8, 32):
        core, z, y_lo = j % 2, (j // 2) % 8, j // 16
        x, y_hi = i % 4, i // 4
        turn = x + 2 * core * x
        return (y_lo + y_hi) % 2 * 16 + (z + turn) % 4 * 2 + 8 * half
    return gy // gx * i + 2 * half


def chunks_of(gx, gy, j, half):
    if (gx, gy) == (8, 32):
        y_lo = j // 16
        return [((y_lo + y_hi) % 2 * 16 + 8 * half, range(4 * y_hi, 4 * y_hi + 4)) for y_hi in range(2)]
    return [(0, range(gx))]


def body(
    gx, gy, n, nz, yb, xb,
    w_hbm, h_hbm, c_hbm, kz_hbm, lk_hbm, ho_hbm,
    w_v, c_v, kz_v, zc, r1, bcat, yo, r2, acat, xo, lk,
    hb, rb, gb, wt, ho, row_out, row_in, col_out, col_in,
    in_sem, c_sem, s1, v1, s2, v2, s3, v3, hs, hv, out_sem,
):
    i = lax.axis_index("gx")
    j = lax.axis_index("gy")
    wide = yb + 2 * PAD
    rows = 2 * yb
    members = range(2)

    w_in = [pltpu.make_async_copy(w_hbm.at[m], w_v.at[m], in_sem.at[m]) for m in members]
    h_in = [
        pltpu.make_async_copy(
            h_hbm.at[m], hb.at[m, :, pl.ds(PAD, yb)], in_sem.at[2 + m]
        )
        for m in members
    ]
    kz_in = pltpu.make_async_copy(kz_hbm, kz_v, c_sem.at[0])
    c_in = pltpu.make_async_copy(c_hbm, c_v, c_sem.at[1])
    kz_in.start()
    w_in[0].start()
    w_in[1].start()
    h_in[0].start()
    h_in[1].start()
    c_in.start()

    barrier = pltpu.get_barrier_semaphore()

    @pl.loop(1, gx)
    def _(k):
        pl.semaphore_signal(barrier, inc=1, device_id=((i + k) % gx, j), device_id_type=MESH)

    @pl.loop(1, gy)
    def _(k):
        pl.semaphore_signal(barrier, inc=1, device_id=(i, (j + k) % gy), device_id_type=MESH)

    def filter_z(m):
        for q in range(yb // 8):
            x = w_v[m, :, 8 * q : 8 * q + 8, :].reshape(nz * 8, xb)
            high, low = split(x)
            p = dot(kz_v[0], jnp.concatenate([high, low], axis=1))
            r = p[:, :xb] + p[:, xb:] + dot(kz_v[1], high)
            zc[m, :, 8 * q : 8 * q + 8, :] = r.reshape(nz, 8, xb)
        r1[m, j] = zc[m, j]

    def copy1(m, k):
        peer = (j + k) % gy
        return pltpu.make_async_remote_copy(
            src_ref=zc.at[m, peer],
            dst_ref=r1.at[m, j],
            send_sem=s1.at[m],
            recv_sem=v1.at[m],
            device_id=(i, peer),
            device_id_type=MESH,
        )

    def send1(m):
        @pl.loop(1, gy)
        def _(k):
            copy1(m, k).start()

    kz_in.wait()
    w_in[0].wait()
    filter_z(0)
    pl.semaphore_wait(barrier, gx + gy - 2)
    send1(0)
    w_in[1].wait()
    filter_z(1)
    send1(1)

    lane = lax.broadcasted_iota(jnp.int32, (yb, xb), 1)
    first, last = lane == 0, lane == xb - 1
    even = lane % 2 == 0
    peers = (
        ((i + gx - 1) % gx, j),
        ((i + 1) % gx, j),
        (i, (j + gy - 1) % gy),
        (i, (j + 1) % gy),
    )

    def edge_copy(field, m, side):
        out, inn = (col_out, col_in) if side < 2 else (row_out, row_in)
        return pltpu.make_async_remote_copy(
            src_ref=out.at[field, m, side % 2],
            dst_ref=inn.at[field, m, side % 2],
            send_sem=hs.at[field, m, side],
            recv_sem=hv.at[field, m, side],
            device_id=peers[side],
            device_id_type=MESH,
        )

    zero = jnp.zeros((yb, xb), F32)

    def pack(field, m, z, x, packed):
        to_left, to_right = packed
        row_out[field, m, 0, pl.ds(z, 1), :] = x[0:1]
        row_out[field, m, 1, pl.ds(z, 1), :] = x[yb - 1 : yb]
        left_at = (2 * z + xb - 1) % xb
        to_left = jnp.where(lane == left_at, pltpu.roll(x, left_at, 1), to_left)
        to_right = jnp.where(lane == 2 * z, pltpu.roll(x, 2 * z + 1, 1), to_right)
        return to_left, to_right

    def send_edges(field, m, packed):
        col_out[field, m, 0] = packed[0]
        col_out[field, m, 1] = packed[1]
        for side in range(4):
            edge_copy(field, m, side).start()

    def take_edges(field, ref, m):
        for side in range(4):
            edge_copy(field, m, side).wait_recv()
        for z in range(nz):
            ref[m, z, PAD + yb : PAD + yb + 1, :] = row_in[field, m, 0, z : z + 1, :]
            ref[m, z, PAD - 1 : PAD, :] = row_in[field, m, 1, z : z + 1, :]
        return jnp.where(even, col_in[field, m, 1], col_in[field, m, 0])

    def own_edges(field, m):
        left = pltpu.roll(col_out[field, m, 0], 1, 1)
        right = pltpu.roll(col_out[field, m, 1], xb - 1, 1)
        return jnp.where(even, left, right)

    for m in members:
        h_in[m].wait()

        def pack_head(z, packed):
            return pack(0, m, z, hb[m, z, PAD : PAD + yb, :], packed)

        send_edges(0, m, lax.fori_loop(0, nz, pack_head, (zero, zero), unroll=16))

    def wait_all(ref, sem):
        pltpu.make_async_copy(ref, ref, sem).wait()

    def copy2(m, half, to):
        return pltpu.make_async_remote_copy(
            src_ref=yo.at[m, pl.ds(blocks_of(gx, gy, to, j, half), 2)],
            dst_ref=r2.at[m, half, i],
            send_sem=s2.at[m, half],
            recv_sem=v2.at[m, half],
            device_id=(to, j),
            device_id_type=MESH,
        )

    def filter_y(m):
        per = 256 // yb
        for s in range(gy):
            high, low = split(r1[m, s])
            bcat[s * yb : (s + 1) * yb, 0:xb] = high
            bcat[s * yb : (s + 1) * yb, xb : 2 * xb] = low
        for turn in range(2):
            half = (j + turn) % 2
            for start, takers in chunks_of(gx, gy, j, half):
                lines = pl.ds(pl.multiple_of(start * yb, 256), 256)
                p = dot(c_v[0, lines, :], bcat[...])
                r = p[:, :xb] + p[:, xb:] + dot(c_v[1, lines, :], bcat[:, 0:xb])
                yo[m, pl.ds(start, per)] = r.reshape(per, yb, xb)
                for to in takers:

                    @pl.when(to != i)
                    def _():
                        copy2(m, half, to).start()

            r2[m, half, i] = yo[m, pl.ds(blocks_of(gx, gy, i, j, half), 2)]

    def copy3(m, half, to, c):
        return pltpu.make_async_remote_copy(
            src_ref=xo.at[m, half, to, c],
            dst_ref=lk.at[m, j],
            send_sem=s3.at[m],
            recv_sem=v3.at[m],
            device_id=(to, blocks_of(gx, gy, i, j, half) + c),
            device_id_type=MESH,
        )

    def each3(m, half, to, here, there):
        for c in range(2):
            own = (to == i) & (blocks_of(gx, gy, i, j, half) + c == j)

            @pl.when(own)
            def _():
                here(m, half, to, c)

            @pl.when(jnp.logical_not(own))
            def _():
                there(m, half, to, c)

    def keep3(m, half, to, c):
        pltpu.make_async_copy(xo.at[m, half, to, c], lk.at[m, j], v3.at[m]).start()

    def filter_x(m):
        for turn in range(2):
            half = (j + turn) % 2
            wait_all(r2.at[m, half, pl.ds(0, gx - 1)], v2.at[m, half])
            for s in range(gx):
                high, low = split(r2[m, half, s].reshape(rows, xb))
                acat[0:rows, s * xb : (s + 1) * xb] = high
                acat[rows : 2 * rows, s * xb : (s + 1) * xb] = low
            for turn_x in range(gx // 2):
                pair = (i // 2 + turn_x) % (gx // 2)
                cols = pl.ds(pl.multiple_of(pair * 2 * xb, 2 * xb), 2 * xb)
                p = dot(acat[...], c_v[0, :, cols])
                r = p[:rows] + p[rows:] + dot(acat[0:rows, :], c_v[1, :, cols])
                for side in range(2):
                    to = 2 * pair + side
                    xo[m, half, to] = r[:, side * xb : (side + 1) * xb].reshape(2, yb, xb)
                    each3(m, half, to, keep3, lambda *at: copy3(*at).start())

    c_in.wait()
    for m in members:
        wait_all(r1.at[m, pl.ds(0, gy - 1)], v1.at[m])
        filter_y(m)
        filter_x(m)

    row_at = yb * j + lax.broadcasted_iota(jnp.int32, (yb, xb), 0)
    col_at = xb * i + lane
    pinned = (row_at == 0) | (row_at == n - 1) | (col_at == 0) | (col_at == n - 1)

    def inverse(x):
        guess = pl.reciprocal(x, approx=True)
        return guess * (2.0 - x * guess)

    def layer(ref, m, z):
        return ref[m, z, PAD : PAD + yb, :]

    def above(ref, m, z):
        return ref[m, z, PAD - 1 : PAD - 1 + yb, :]

    def under(ref, m, z):
        return ref[m, z, PAD + 1 : PAD + 1 + yb, :]

    def to_lane(packed, z):
        return pltpu.roll(packed, (xb - 2 * z) % xb, 1)

    def flow_x(w, h, edge_w, edge_h, z):
        right = jnp.where(last, to_lane(edge_w, z), w)
        w_left = jnp.where(first, to_lane(edge_w, z), pltpu.roll(w, 1, 1))
        e = to_lane(edge_h, z)
        h_right = jnp.where(last, e, pltpu.roll(h, xb - 1, 1))
        h_left = jnp.where(first, e, pltpu.roll(h, 1, 1))
        return right * h_right + w_left * h_left, right + w_left

    def resist(m):
        wait_all(lk.at[m], v3.at[m])
        pltpu.make_async_copy(lk.at[m], lk_hbm.at[m], out_sem.at[m]).start()

        def step(z, packed):
            r = jnp.exp(-lk[m, z])
            rb[m, z, PAD : PAD + yb, :] = r
            return pack(1, m, z, r, packed)

        send_edges(1, m, lax.fori_loop(0, nz, step, (zero, zero), unroll=True))
        for z in (0, nz - 1):
            gb[m, z, PAD : PAD + yb, :] = layer(hb, m, z)
            ho[m, z] = layer(hb, m, z)

    def first_sweep(m):
        h_edge = take_edges(0, hb, m)
        r_edge = take_edges(1, rb, m)
        w_edge = inverse(own_edges(1, m) + r_edge)

        def step(z, carry):
            r, h_low, h, w_low, packed = carry
            r_high = layer(rb, m, z + 1)
            h_high = layer(hb, m, z + 1)
            w_high = inverse(r + r_high)
            w_up = inverse(r + above(rb, m, z))
            w_down = inverse(r + under(rb, m, z))
            w_x = inverse(r + pltpu.roll(r, xb - 1, 1))
            gain, total = flow_x(w_x, h, w_edge, h_edge, z)
            total = total + ((w_low + w_high) + (w_up + w_down))
            gain = gain + (w_low * h_low + w_high * h_high)
            gain = gain + (w_up * above(hb, m, z) + w_down * under(hb, m, z))
            share = inverse(total)
            new = jnp.where(pinned, h, gain * share)
            gb[m, z, PAD : PAD + yb, :] = new
            wt[m, 0, z] = w_x
            wt[m, 1, z] = w_high
            wt[m, 2, z] = w_up
            wt[m, 3, z] = w_down
            wt[m, 4, z] = share
            return r_high, h, h_high, w_high, pack(2, m, z, new, packed)

        r0, r1_ = layer(rb, m, 0), layer(rb, m, 1)
        w_first = inverse(r0 + r1_)
        wt[m, 1, 0] = w_first
        start = (r1_, layer(hb, m, 0), layer(hb, m, 1), w_first, (zero, zero))
        send_edges(2, m, lax.fori_loop(1, nz - 1, step, start, unroll=6)[-1])
        return w_edge

    def second_sweep(m, w_edge):
        g_edge = take_edges(2, gb, m)

        def step(z, carry):
            h_low, h, w_low = carry
            h_high = layer(gb, m, z + 1)
            w_high = wt[m, 1, z]
            gain, _ = flow_x(wt[m, 0, z], h, w_edge, g_edge, z)
            gain = gain + (w_low * h_low + w_high * h_high)
            gain = gain + (wt[m, 2, z] * above(gb, m, z) + wt[m, 3, z] * under(gb, m, z))
            ho[m, z] = jnp.where(pinned, h, gain * wt[m, 4, z])
            return h, h_high, w_high

        start = (layer(gb, m, 0), layer(gb, m, 1), wt[m, 1, 0])
        lax.fori_loop(1, nz - 1, step, start, unroll=10)
        pltpu.make_async_copy(ho.at[m], ho_hbm.at[m], out_sem.at[2 + m]).start()

    for m in members:
        resist(m)
    w_edges = [first_sweep(m) for m in members]
    for m in members:
        second_sweep(m, w_edges[m])

    for m in members:
        pltpu.make_async_copy(lk.at[m], lk_hbm.at[m], out_sem.at[m]).wait()
        pltpu.make_async_copy(ho.at[m], ho_hbm.at[m], out_sem.at[2 + m]).wait()
        for field in range(3):
            for side in range(4):
                edge_copy(field, m, side).wait_send()

        @pl.loop(1, gy)
        def _(k):
            copy1(m, k).wait_send()

        for half in range(2):

            @pl.loop(1, gx)
            def _(k):
                copy2(m, half, (i + k) % gx).wait_send()

            @pl.loop(0, gx)
            def _(to):
                each3(m, half, to, lambda *at: None, lambda *at: copy3(*at).wait_send())


def on_device(gx, gy, white_noise, head_start):
    _, nz, yb, xb = white_noise.shape
    n = yb * gy
    assert n == xb * gx
    assert n == 4 * yb * gx and nz == gy
    rows = 2 * yb
    wide = yb + 2 * PAD
    matrix = jnp.asarray(split_pair(circulant(n)))
    z_matrix = jnp.asarray(split_pair(np.kron(circulant(nz), np.eye(8))))
    block = jax.ShapeDtypeStruct(white_noise.shape, F32)
    dma = pltpu.SemaphoreType.DMA
    results = pl.pallas_call(
        functools.partial(body, gx, gy, n, nz, yb, xb),
        out_shape=(pltpu.VMEM(block.shape, F32),) * 2,
        in_specs=[pl.BlockSpec(memory_space=pl.ANY)] * 4,
        out_specs=(pl.BlockSpec(memory_space=pl.ANY),) * 2,
        scratch_shapes=[
            pltpu.VMEM((2, nz, yb, xb), F32),
            pltpu.VMEM((2, n, n), BF16),
            pltpu.VMEM((2, nz * 8, nz * 8), BF16),
            pltpu.VMEM((2, nz, yb, xb), F32),
            pltpu.VMEM((2, gy, yb, xb), F32),
            pltpu.VMEM((n, 2 * xb), BF16),
            pltpu.VMEM((2, gy, yb, xb), F32),
            pltpu.VMEM((2, 2, gx, 2, yb, xb), F32),
            pltpu.VMEM((2 * rows, n), BF16),
            pltpu.VMEM((2, 2, gx, 2, yb, xb), F32),
            pltpu.VMEM((2, nz, yb, xb), F32),
            pltpu.VMEM((2, nz, wide, xb), F32),
            pltpu.VMEM((2, nz, wide, xb), F32),
            pltpu.VMEM((2, nz, wide, xb), F32),
            pltpu.VMEM((2, 5, nz, yb, xb), F32),
            pltpu.VMEM((2, nz, yb, xb), F32),
            pltpu.VMEM((3, 2, 2, nz, xb), F32),
            pltpu.VMEM((3, 2, 2, nz, xb), F32),
            pltpu.VMEM((3, 2, 2, yb, xb), F32),
            pltpu.VMEM((3, 2, 2, yb, xb), F32),
            dma((4,)),
            dma((2,)),
            dma((2,)), dma((2,)),
            dma((2, 2)), dma((2, 2)),
            dma((2,)), dma((2,)),
            dma((3, 2, 4)), dma((3, 2, 4)),
            dma((4,)),
        ],
        compiler_params=pltpu.CompilerParams(
            collective_id=0, has_side_effects=True, vmem_limit_bytes=60 * 1024 * 1024
        ),
        cost_estimate=pl.CostEstimate(
            flops=12 * 2 * rows * 2 * n * n, bytes_accessed=16 * n * xb * 4, transcendentals=2 * nz * yb * xb
        ),
    )(white_noise, head_start, matrix, z_matrix)
    return results


def solution(mesh):
    spec = P(None, None, "gy", "gx")
    return jax.shard_map(
        functools.partial(on_device, mesh.shape["gx"], mesh.shape["gy"]),
        mesh=mesh,
        in_specs=(spec, spec),
        out_specs=(spec, spec),
        check_vma=False,
    )
```

```python
import functools
import math

import jax
import jax.numpy as jnp
import ml_dtypes
import numpy as np
from jax import lax
from jax.experimental import pallas as pl
from jax.experimental.pallas import tpu as pltpu
from jax.sharding import PartitionSpec as P

F32 = jnp.float32
BF16 = jnp.bfloat16
MESH = pl.DeviceIdType.MESH
PAD = 8


def circulant(length):
    k = np.arange(length)
    q = np.minimum(k, length - k)
    w = 2.0 * math.pi * q / length
    s = 1.0 / (1.0 + (w * (length / 16.0)) ** 2)
    a = np.sqrt(s / np.mean(s))
    taps = np.real(np.fft.ifft(a))
    return taps[(k[:, None] - k[None, :]) % length]


def split_pair(matrix):
    high = matrix.astype(ml_dtypes.bfloat16)
    low = (matrix - high.astype(np.float64)).astype(ml_dtypes.bfloat16)
    return np.stack([high, low])


def split(x):
    high = x.astype(BF16)
    low = (x - high.astype(F32)).astype(BF16)
    return high, low


def dot(a, b):
    return jnp.dot(a, b, preferred_element_type=F32)


def blocks_of(gx, gy, i, j, half):
    if (gx, gy) == (8, 32):
        core, z, y_lo = j % 2, (j // 2) % 8, j // 16
        x, y_hi = i % 4, i // 4
        turn = x + 2 * core * x
        return (y_lo + y_hi) % 2 * 16 + (z + turn) % 4 * 2 + 8 * half
    return gy // gx * i + 2 * half


def chunks_of(gx, gy, j, half):
    if (gx, gy) == (8, 32):
        y_lo = j // 16
        return [((y_lo + y_hi) % 2 * 16 + 8 * half, range(4 * y_hi, 4 * y_hi + 4)) for y_hi in range(2)]
    return [(0, range(gx))]


def body(
    gx, gy, n, nz, yb, xb,
    w_hbm, h_hbm, c_hbm, kz_hbm, lk_hbm, ho_hbm,
    w_v, c_v, kz_v, zc, r1, bcat, yo, r2, acat, xo, lk,
    hb, rb, gb, wt, ho, row_out, row_in, cols, col_in, corner_in,
    in_sem, c_sem, s1, v1, s2, v2, s3, v3, hs, hv, out_sem,
):
    i = lax.axis_index("gx")
    j = lax.axis_index("gy")
    wide = yb + 2 * PAD
    rows = 2 * yb
    members = range(2)

    w_in = [pltpu.make_async_copy(w_hbm.at[m], w_v.at[m], in_sem.at[m]) for m in members]
    h_in = [
        pltpu.make_async_copy(
            h_hbm.at[m], hb.at[m, :, pl.ds(PAD, yb)], in_sem.at[2 + m]
        )
        for m in members
    ]
    kz_in = pltpu.make_async_copy(kz_hbm, kz_v, c_sem.at[0])
    c_in = pltpu.make_async_copy(c_hbm, c_v, c_sem.at[1])
    kz_in.start()
    w_in[0].start()
    w_in[1].start()
    h_in[0].start()
    h_in[1].start()
    c_in.start()

    barrier = pltpu.get_barrier_semaphore()

    @pl.loop(1, gx)
    def _(k):
        pl.semaphore_signal(barrier, inc=1, device_id=((i + k) % gx, j), device_id_type=MESH)

    @pl.loop(1, gy)
    def _(k):
        pl.semaphore_signal(barrier, inc=1, device_id=(i, (j + k) % gy), device_id_type=MESH)

    diagonal = [((i + (gx - 1, 1)[cs]) % gx, (j + (gy - 1, 1)[rs]) % gy) for cs in range(2) for rs in range(2)]
    for peer in diagonal:
        pl.semaphore_signal(barrier, inc=1, device_id=peer, device_id_type=MESH)

    def filter_z(m):
        for q in range(yb // 8):
            x = w_v[m, :, 8 * q : 8 * q + 8, :].reshape(nz * 8, xb)
            high, low = split(x)
            p = dot(kz_v[0], jnp.concatenate([high, low], axis=1))
            r = p[:, :xb] + p[:, xb:] + dot(kz_v[1], high)
            zc[m, :, 8 * q : 8 * q + 8, :] = r.reshape(nz, 8, xb)
        r1[m, j] = zc[m, j]

    def copy1(m, k):
        peer = (j + k) % gy
        return pltpu.make_async_remote_copy(
            src_ref=zc.at[m, peer],
            dst_ref=r1.at[m, j],
            send_sem=s1.at[m],
            recv_sem=v1.at[m],
            device_id=(i, peer),
            device_id_type=MESH,
        )

    def send1(m):
        @pl.loop(1, gy)
        def _(k):
            copy1(m, k).start()

    kz_in.wait()
    w_in[0].wait()
    filter_z(0)
    pl.semaphore_wait(barrier, gx + gy + 2)
    send1(0)
    w_in[1].wait()
    filter_z(1)
    send1(1)

    lane = lax.broadcasted_iota(jnp.int32, (yb, xb), 1)
    first, last = lane == 0, lane == xb - 1
    even = lane % 2 == 0
    layer_0 = lane // 2
    layer_1 = jnp.where(even, lane // 2 - 1, (lane + 1) % xb // 2)
    around = (
        ((i + gx - 1) % gx, j),
        ((i + 1) % gx, j),
        (i, (j + gy - 1) % gy),
        (i, (j + 1) % gy),
        *diagonal,
    )

    def edge_copy(field, m, at):
        if at < 2:
            source, target = cols.at[field, m], col_in.at[field, m, at]
        elif at < 4:
            source, target = row_out.at[field, m, at - 2], row_in.at[field, m, at - 2]
        else:
            start = (0, yb - 8)[at % 2]
            source = cols.at[field, m, 0, pl.ds(start, 8)]
            target = corner_in.at[field, m, at - 4]
        return pltpu.make_async_remote_copy(
            src_ref=source,
            dst_ref=target,
            send_sem=hs.at[field, m, at],
            recv_sem=hv.at[field, m, at],
            device_id=around[at],
            device_id_type=MESH,
        )

    zero = jnp.zeros((yb, xb), F32)

    def pack(field, m, z, x, packed):
        for side, at in enumerate((0, yb - 1)):
            inner = (1, yb - 2)[side]
            row_out[field, m, side, 0, pl.ds(z, 1), :] = x[at : at + 1]
            row_out[field, m, side, 1, pl.ds(z, 1), :] = x[inner : inner + 1]
        turned = pltpu.roll(x, 2 * z + 1, 1)
        return (
            jnp.where(layer_0 == z, turned, packed[0]),
            jnp.where(layer_1 == z, turned, packed[1]),
        )

    def send_edges(field, m, packed):
        cols[field, m, 0] = packed[0]
        cols[field, m, 1] = packed[1]
        for at in range(8):
            edge_copy(field, m, at).start()

    def to_left(x, by):
        return pltpu.roll(x, x.shape[1] - by, 1)

    def take_edges(field, ref, m):
        for at in range(8):
            edge_copy(field, m, at).wait_recv()
        if ref is not None:
            for z in range(nz):
                ref[m, z, PAD + yb : PAD + yb + 1, :] = row_in[field, m, 0, 0, z : z + 1, :]
                ref[m, z, PAD - 1 : PAD, :] = row_in[field, m, 1, 0, z : z + 1, :]
        beside = jnp.where(even, col_in[field, m, 1, 0], to_left(col_in[field, m, 0, 0], 2))
        beyond = jnp.where(
            even, pltpu.roll(col_in[field, m, 1, 1], 1, 1), to_left(col_in[field, m, 0, 1], 3)
        )
        own = to_left(cols[field, m, 0], 1)
        tile_even = even[0:8]

        def corner(rs, at):
            left, right = corner_in[field, m, 2 + rs], to_left(corner_in[field, m, rs], 2)
            return jnp.where(tile_even, left, right)[at : at + 1]

        return beside, beyond, own, corner(1, 7), corner(0, 0)

    for m in members:
        h_in[m].wait()

        def pack_head(z, packed):
            return pack(0, m, z, hb[m, z, PAD : PAD + yb, :], packed)

        send_edges(0, m, lax.fori_loop(0, nz, pack_head, (zero, zero), unroll=True))

    def wait_all(ref, sem):
        pltpu.make_async_copy(ref, ref, sem).wait()

    def copy2(m, half, to):
        return pltpu.make_async_remote_copy(
            src_ref=yo.at[m, pl.ds(blocks_of(gx, gy, to, j, half), 2)],
            dst_ref=r2.at[m, half, i],
            send_sem=s2.at[m, half],
            recv_sem=v2.at[m, half],
            device_id=(to, j),
            device_id_type=MESH,
        )

    def filter_y(m):
        per = 256 // yb
        for s in range(gy):
            high, low = split(r1[m, s])
            bcat[s * yb : (s + 1) * yb, 0:xb] = high
            bcat[s * yb : (s + 1) * yb, xb : 2 * xb] = low
        for turn in range(2):
            half = (j + turn) % 2
            for start, takers in chunks_of(gx, gy, j, half):
                lines = pl.ds(pl.multiple_of(start * yb, 256), 256)
                p = dot(c_v[0, lines, :], bcat[...])
                r = p[:, :xb] + p[:, xb:] + dot(c_v[1, lines, :], bcat[:, 0:xb])
                yo[m, pl.ds(start, per)] = r.reshape(per, yb, xb)
                for to in takers:

                    @pl.when(to != i)
                    def _():
                        copy2(m, half, to).start()

            r2[m, half, i] = yo[m, pl.ds(blocks_of(gx, gy, i, j, half), 2)]

    def copy3(m, half, to, c):
        return pltpu.make_async_remote_copy(
            src_ref=xo.at[m, half, to, c],
            dst_ref=lk.at[m, j],
            send_sem=s3.at[m],
            recv_sem=v3.at[m],
            device_id=(to, blocks_of(gx, gy, i, j, half) + c),
            device_id_type=MESH,
        )

    def each3(m, half, to, here, there):
        for c in range(2):
            own = (to == i) & (blocks_of(gx, gy, i, j, half) + c == j)

            @pl.when(own)
            def _():
                here(m, half, to, c)

            @pl.when(jnp.logical_not(own))
            def _():
                there(m, half, to, c)

    def keep3(m, half, to, c):
        pltpu.make_async_copy(xo.at[m, half, to, c], lk.at[m, j], v3.at[m]).start()

    def filter_x(m):
        for turn in range(2):
            half = (j + turn) % 2
            wait_all(r2.at[m, half, pl.ds(0, gx - 1)], v2.at[m, half])
            for s in range(gx):
                high, low = split(r2[m, half, s].reshape(rows, xb))
                acat[0:rows, s * xb : (s + 1) * xb] = high
                acat[rows : 2 * rows, s * xb : (s + 1) * xb] = low
            for turn_x in range(gx // 2):
                pair = (i // 2 + turn_x) % (gx // 2)
                cols = pl.ds(pl.multiple_of(pair * 2 * xb, 2 * xb), 2 * xb)
                p = dot(acat[...], c_v[0, :, cols])
                r = p[:rows] + p[rows:] + dot(acat[0:rows, :], c_v[1, :, cols])
                for side in range(2):
                    to = 2 * pair + side
                    xo[m, half, to] = r[:, side * xb : (side + 1) * xb].reshape(2, yb, xb)
                    each3(m, half, to, keep3, lambda *at: copy3(*at).start())

    c_in.wait()
    for m in members:
        wait_all(r1.at[m, pl.ds(0, gy - 1)], v1.at[m])
        filter_y(m)
        filter_x(m)

    row_at = yb * j + lax.broadcasted_iota(jnp.int32, (yb, xb), 0)
    col_at = xb * i + lane
    pinned = (row_at == 0) | (row_at == n - 1) | (col_at == 0) | (col_at == n - 1)

    def inverse(x):
        guess = pl.reciprocal(x, approx=True)
        return guess * (2.0 - x * guess)

    def layer(ref, m, z):
        return ref[m, z, PAD : PAD + yb, :]

    def above(ref, m, z):
        return ref[m, z, PAD - 1 : PAD - 1 + yb, :]

    def under(ref, m, z):
        return ref[m, z, PAD + 1 : PAD + 1 + yb, :]

    def to_lane(packed, z):
        return pltpu.roll(packed, (xb - 2 * z) % xb, 1)

    def flow_x(w, h, edge_w, edge_h, z):
        right = jnp.where(last, to_lane(edge_w, z), w)
        w_left = jnp.where(first, to_lane(edge_w, z), pltpu.roll(w, 1, 1))
        e = to_lane(edge_h, z)
        h_right = jnp.where(last, e, pltpu.roll(h, xb - 1, 1))
        h_left = jnp.where(first, e, pltpu.roll(h, 1, 1))
        return right * h_right + w_left * h_left, right + w_left

    def resist(m):
        wait_all(lk.at[m], v3.at[m])
        pltpu.make_async_copy(lk.at[m], lk_hbm.at[m], out_sem.at[m]).start()

        def step(z, packed):
            r = jnp.exp(-lk[m, z])
            rb[m, z, PAD : PAD + yb, :] = r
            return pack(1, m, z, r, packed)

        send_edges(1, m, lax.fori_loop(0, nz, step, (zero, zero), unroll=True))
        for z in (0, nz - 1):
            gb[m, z, PAD : PAD + yb, :] = layer(hb, m, z)
            ho[m, z] = layer(hb, m, z)

    row_of = lax.broadcasted_iota(jnp.int32, (yb, xb), 0)
    z_of = lax.broadcasted_iota(jnp.int32, (nz, xb), 0)
    z_lane = lax.broadcasted_iota(jnp.int32, (nz, xb), 1)
    z_col = xb * i + z_lane
    row_pinned = (z_of == 0) | (z_of == nz - 1) | (z_col == 0) | (z_col == n - 1)
    top = 2 * nz - 2
    col_pinned = (row_at == 0) | (row_at == n - 1) | first | last | (lane == top) | (lane == top - 1)

    def relaxed(r, h, pairs, kept):
        weights = [inverse(r + r_beside) for r_beside, _ in pairs]
        total = sum(weights[1:], weights[0])
        gain = sum(w * h_beside for w, (_, h_beside) in zip(weights, pairs))
        return jnp.where(kept, h, gain * inverse(total))

    def ring(m, r_edges, h_edges):
        def along_rows(edges, field, side):
            beside, beyond = row_in[field, m, 1 - side, 0], row_in[field, m, 1 - side, 1]
            corners = edges[3 + side]
            pick = lambda at: jnp.sum(jnp.where(z_lane == at, corners, 0.0), axis=1, keepdims=True)
            left, right = pick(2 * z_of), pick((2 * z_of + xb - 1) % xb)
            return beside, (
                beyond,
                row_out[field, m, side, 0],
                jnp.where(z_lane == 0, left, pltpu.roll(beside, 1, 1)),
                jnp.where(z_lane == xb - 1, right, pltpu.roll(beside, xb - 1, 1)),
                pltpu.roll(beside, 1, 0),
                pltpu.roll(beside, nz - 1, 0),
            )

        for side in range(2):
            r, r_pairs = along_rows(r_edges, 1, side)
            h, h_pairs = along_rows(h_edges, 0, side)
            new = relaxed(r, h, list(zip(r_pairs, h_pairs)), row_pinned)
            at = (PAD - 1, PAD + yb)[side]
            for z in range(nz):
                gb[m, z, at : at + 1, :] = new[z : z + 1]

        def along_cols(edges):
            beside, beyond, own, up, down = edges
            return beside, (
                beyond,
                own,
                jnp.where(row_of == 0, up, pltpu.roll(beside, 1, 0)),
                jnp.where(row_of == yb - 1, down, pltpu.roll(beside, yb - 1, 0)),
                pltpu.roll(beside, 2, 1),
                pltpu.roll(beside, xb - 2, 1),
            )

        r, r_pairs = along_cols(r_edges)
        h, h_pairs = along_cols(h_edges)
        return relaxed(r, h, list(zip(r_pairs, h_pairs)), col_pinned)

    def sweeps(m):
        h_edges = take_edges(0, hb, m)
        r_edges = take_edges(1, rb, m)
        h_edge = h_edges[0]
        w_edge = inverse(r_edges[2] + r_edges[0])
        g_edge = ring(m, r_edges, h_edges)

        def step(z, carry):
            r, h_low, h, w_low = carry
            r_high = layer(rb, m, z + 1)
            h_high = layer(hb, m, z + 1)
            w_high = inverse(r + r_high)
            w_up = inverse(r + above(rb, m, z))
            w_down = inverse(r + under(rb, m, z))
            w_x = inverse(r + pltpu.roll(r, xb - 1, 1))
            gain, total = flow_x(w_x, h, w_edge, h_edge, z)
            total = total + ((w_low + w_high) + (w_up + w_down))
            gain = gain + (w_low * h_low + w_high * h_high)
            gain = gain + (w_up * above(hb, m, z) + w_down * under(hb, m, z))
            share = inverse(total)
            gb[m, z, PAD : PAD + yb, :] = jnp.where(pinned, h, gain * share)
            wt[0, z] = w_x
            wt[1, z] = w_high
            wt[2, z] = w_up
            wt[3, z] = w_down
            wt[4, z] = share
            return r_high, h, h_high, w_high

        r0, r1_ = layer(rb, m, 0), layer(rb, m, 1)
        w_first = inverse(r0 + r1_)
        start = (r1_, layer(hb, m, 0), layer(hb, m, 1), w_first)
        lax.fori_loop(1, nz - 1, step, start, unroll=6)

        def again(z, carry):
            h_low, h, w_low = carry
            h_high = layer(gb, m, z + 1)
            w_high = wt[1, z]
            gain, _ = flow_x(wt[0, z], h, w_edge, g_edge, z)
            gain = gain + (w_low * h_low + w_high * h_high)
            gain = gain + (wt[2, z] * above(gb, m, z) + wt[3, z] * under(gb, m, z))
            ho[m, z] = jnp.where(pinned, h, gain * wt[4, z])
            return h, h_high, w_high

        start = (layer(gb, m, 0), layer(gb, m, 1), w_first)
        lax.fori_loop(1, nz - 1, again, start, unroll=10)
        pltpu.make_async_copy(ho.at[m], ho_hbm.at[m], out_sem.at[2 + m]).start()

    for m in members:
        resist(m)
    for m in members:
        sweeps(m)

    for m in members:
        pltpu.make_async_copy(lk.at[m], lk_hbm.at[m], out_sem.at[m]).wait()
        pltpu.make_async_copy(ho.at[m], ho_hbm.at[m], out_sem.at[2 + m]).wait()
        for field in range(2):
            for at in range(8):
                edge_copy(field, m, at).wait_send()

        @pl.loop(1, gy)
        def _(k):
            copy1(m, k).wait_send()

        for half in range(2):

            @pl.loop(1, gx)
            def _(k):
                copy2(m, half, (i + k) % gx).wait_send()

            @pl.loop(0, gx)
            def _(to):
                each3(m, half, to, lambda *at: None, lambda *at: copy3(*at).wait_send())


def on_device(gx, gy, white_noise, head_start):
    _, nz, yb, xb = white_noise.shape
    n = yb * gy
    assert n == xb * gx
    assert n == 4 * yb * gx and nz == gy
    rows = 2 * yb
    wide = yb + 2 * PAD
    matrix = jnp.asarray(split_pair(circulant(n)))
    z_matrix = jnp.asarray(split_pair(np.kron(circulant(nz), np.eye(8))))
    block = jax.ShapeDtypeStruct(white_noise.shape, F32)
    dma = pltpu.SemaphoreType.DMA
    results = pl.pallas_call(
        functools.partial(body, gx, gy, n, nz, yb, xb),
        out_shape=(pltpu.VMEM(block.shape, F32),) * 2,
        in_specs=[pl.BlockSpec(memory_space=pl.ANY)] * 4,
        out_specs=(pl.BlockSpec(memory_space=pl.ANY),) * 2,
        scratch_shapes=[
            pltpu.VMEM((2, nz, yb, xb), F32),
            pltpu.VMEM((2, n, n), BF16),
            pltpu.VMEM((2, nz * 8, nz * 8), BF16),
            pltpu.VMEM((2, nz, yb, xb), F32),
            pltpu.VMEM((2, gy, yb, xb), F32),
            pltpu.VMEM((n, 2 * xb), BF16),
            pltpu.VMEM((2, gy, yb, xb), F32),
            pltpu.VMEM((2, 2, gx, 2, yb, xb), F32),
            pltpu.VMEM((2 * rows, n), BF16),
            pltpu.VMEM((2, 2, gx, 2, yb, xb), F32),
            pltpu.VMEM((2, nz, yb, xb), F32),
            pltpu.VMEM((2, nz, wide, xb), F32),
            pltpu.VMEM((2, nz, wide, xb), F32),
            pltpu.VMEM((2, nz, wide, xb), F32),
            pltpu.VMEM((5, nz, yb, xb), F32),
            pltpu.VMEM((2, nz, yb, xb), F32),
            pltpu.VMEM((2, 2, 2, 2, nz, xb), F32),
            pltpu.VMEM((2, 2, 2, 2, nz, xb), F32),
            pltpu.VMEM((2, 2, 2, yb, xb), F32),
            pltpu.VMEM((2, 2, 2, 2, yb, xb), F32),
            pltpu.VMEM((2, 2, 4, 8, xb), F32),
            dma((4,)),
            dma((2,)),
            dma((2,)), dma((2,)),
            dma((2, 2)), dma((2, 2)),
            dma((2,)), dma((2,)),
            dma((2, 2, 8)), dma((2, 2, 8)),
            dma((4,)),
        ],
        compiler_params=pltpu.CompilerParams(
            collective_id=0, has_side_effects=True, vmem_limit_bytes=60 * 1024 * 1024
        ),
        cost_estimate=pl.CostEstimate(
            flops=12 * 2 * rows * 2 * n * n, bytes_accessed=16 * n * xb * 4, transcendentals=2 * nz * yb * xb
        ),
    )(white_noise, head_start, matrix, z_matrix)
    return results


def solution(mesh):
    spec = P(None, None, "gy", "gx")
    return jax.shard_map(
        functools.partial(on_device, mesh.shape["gx"], mesh.shape["gy"]),
        mesh=mesh,
        in_specs=(spec, spec),
        out_specs=(spec, spec),
        check_vma=False,
    )
```

```python
import functools
import math

import jax
import jax.numpy as jnp
import ml_dtypes
import numpy as np
from jax import lax
from jax.experimental import pallas as pl
from jax.experimental.pallas import tpu as pltpu
from jax.sharding import PartitionSpec as P

F32 = jnp.float32
BF16 = jnp.bfloat16
MESH = pl.DeviceIdType.MESH
PAD = 8


def circulant(length):
    k = np.arange(length)
    q = np.minimum(k, length - k)
    w = 2.0 * math.pi * q / length
    s = 1.0 / (1.0 + (w * (length / 16.0)) ** 2)
    a = np.sqrt(s / np.mean(s))
    taps = np.real(np.fft.ifft(a))
    return taps[(k[:, None] - k[None, :]) % length]


def split_pair(matrix):
    high = matrix.astype(ml_dtypes.bfloat16)
    low = (matrix - high.astype(np.float64)).astype(ml_dtypes.bfloat16)
    return np.stack([high, low])


def split(x):
    high = x.astype(BF16)
    low = (x - high.astype(F32)).astype(BF16)
    return high, low


def dot(a, b):
    return jnp.dot(a, b, preferred_element_type=F32)


def blocks_of(gx, gy, i, j, half):
    if (gx, gy) == (8, 32):
        core, z, y_lo = j % 2, (j // 2) % 8, j // 16
        x, y_hi = i % 4, i // 4
        turn = x + 2 * core * x
        return (y_lo + y_hi) % 2 * 16 + (z + turn) % 4 * 2 + 8 * half
    return gy // gx * i + 2 * half


def chunks_of(gx, gy, j, half):
    if (gx, gy) == (8, 32):
        y_lo = j // 16
        return [((y_lo + y_hi) % 2 * 16 + 8 * half, range(4 * y_hi, 4 * y_hi + 4)) for y_hi in range(2)]
    return [(0, range(gx))]


def body(
    gx, gy, n, nz, yb, xb,
    w_hbm, h_hbm, c_hbm, kz_hbm, lk_hbm, ho_hbm,
    w_v, c_v, kz_v, zc, r1, bcat, yo, r2, acat, xo, lk,
    hb, rb, gb, wt, ho, row_out, row_in, cols, col_in, corner_in,
    in_sem, c_sem, s1, v1, s2, v2, s3, v3, hs, hv, out_sem,
):
    i = lax.axis_index("gx")
    j = lax.axis_index("gy")
    wide = yb + 2 * PAD
    rows = 2 * yb
    members = range(2)

    w_in = [pltpu.make_async_copy(w_hbm.at[m], w_v.at[m], in_sem.at[m]) for m in members]
    h_in = [
        pltpu.make_async_copy(
            h_hbm.at[m], hb.at[m, :, pl.ds(PAD, yb)], in_sem.at[2 + m]
        )
        for m in members
    ]
    kz_in = pltpu.make_async_copy(kz_hbm, kz_v, c_sem.at[0])
    c_in = pltpu.make_async_copy(c_hbm, c_v, c_sem.at[1])
    kz_in.start()
    w_in[0].start()

    barrier = pltpu.get_barrier_semaphore()

    @pl.loop(1, gx)
    def _(k):
        pl.semaphore_signal(barrier, inc=1, device_id=((i + k) % gx, j), device_id_type=MESH)

    @pl.loop(1, gy)
    def _(k):
        pl.semaphore_signal(barrier, inc=1, device_id=(i, (j + k) % gy), device_id_type=MESH)

    diagonal = [((i + (gx - 1, 1)[cs]) % gx, (j + (gy - 1, 1)[rs]) % gy) for cs in range(2) for rs in range(2)]
    for peer in diagonal:
        pl.semaphore_signal(barrier, inc=1, device_id=peer, device_id_type=MESH)

    w_in[1].start()
    h_in[0].start()
    h_in[1].start()
    c_in.start()

    def filter_z(m):
        for q in range(yb // 8):
            x = w_v[m, :, 8 * q : 8 * q + 8, :].reshape(nz * 8, xb)
            high, low = split(x)
            p = dot(kz_v[0], jnp.concatenate([high, low], axis=1))
            r = p[:, :xb] + p[:, xb:] + dot(kz_v[1], high)
            zc[m, :, 8 * q : 8 * q + 8, :] = r.reshape(nz, 8, xb)
        r1[m, j] = zc[m, j]

    def copy1(m, k):
        peer = (j + k) % gy
        return pltpu.make_async_remote_copy(
            src_ref=zc.at[m, peer],
            dst_ref=r1.at[m, j],
            send_sem=s1.at[m],
            recv_sem=v1.at[m],
            device_id=(i, peer),
            device_id_type=MESH,
        )

    def send1(m):
        @pl.loop(1, gy)
        def _(k):
            copy1(m, k).start()

    kz_in.wait()
    w_in[0].wait()
    filter_z(0)
    pl.semaphore_wait(barrier, gx + gy + 2)
    send1(0)
    w_in[1].wait()
    filter_z(1)

    @pl.loop(1, gy)
    def _(k):
        copy1(0, k).wait_send()

    send1(1)

    lane = lax.broadcasted_iota(jnp.int32, (yb, xb), 1)
    first, last = lane == 0, lane == xb - 1
    even = lane % 2 == 0
    layer_0 = lane // 2
    layer_1 = jnp.where(even, lane // 2 - 1, (lane + 1) % xb // 2)
    around = (
        ((i + gx - 1) % gx, j),
        ((i + 1) % gx, j),
        (i, (j + gy - 1) % gy),
        (i, (j + 1) % gy),
        *diagonal,
    )

    def edge_copy(field, m, at):
        if at < 2:
            source, target = cols.at[field, m], col_in.at[field, m, at]
        elif at < 4:
            source, target = row_out.at[field, m, at - 2], row_in.at[field, m, at - 2]
        else:
            start = (0, yb - 8)[at % 2]
            source = cols.at[field, m, 0, pl.ds(start, 8)]
            target = corner_in.at[field, m, at - 4]
        return pltpu.make_async_remote_copy(
            src_ref=source,
            dst_ref=target,
            send_sem=hs.at[field, m, at],
            recv_sem=hv.at[field, m, at],
            device_id=around[at],
            device_id_type=MESH,
        )

    zero = jnp.zeros((yb, xb), F32)

    def pack(field, m, z, x, packed):
        for side, at in enumerate((0, yb - 1)):
            inner = (1, yb - 2)[side]
            row_out[field, m, side, 0, pl.ds(z, 1), :] = x[at : at + 1]
            row_out[field, m, side, 1, pl.ds(z, 1), :] = x[inner : inner + 1]
        turned = pltpu.roll(x, 2 * z + 1, 1)
        return (
            jnp.where(layer_0 == z, turned, packed[0]),
            jnp.where(layer_1 == z, turned, packed[1]),
        )

    def send_edges(field, m, packed):
        cols[field, m, 0] = packed[0]
        cols[field, m, 1] = packed[1]
        for at in range(8):
            edge_copy(field, m, at).start()

    def to_left(x, by):
        return pltpu.roll(x, x.shape[1] - by, 1)

    def take_edges(field, ref, m):
        for at in range(8):
            edge_copy(field, m, at).wait_recv()
        if ref is not None:
            for z in range(nz):
                ref[m, z, PAD + yb : PAD + yb + 1, :] = row_in[field, m, 0, 0, z : z + 1, :]
                ref[m, z, PAD - 1 : PAD, :] = row_in[field, m, 1, 0, z : z + 1, :]
        beside = jnp.where(even, col_in[field, m, 1, 0], to_left(col_in[field, m, 0, 0], 2))
        beyond = jnp.where(
            even, pltpu.roll(col_in[field, m, 1, 1], 1, 1), to_left(col_in[field, m, 0, 1], 3)
        )
        own = to_left(cols[field, m, 0], 1)
        tile_even = even[0:8]

        def corner(rs, at):
            left, right = corner_in[field, m, 2 + rs], to_left(corner_in[field, m, rs], 2)
            return jnp.where(tile_even, left, right)[at : at + 1]

        return beside, beyond, own, corner(1, 7), corner(0, 0)

    for m in members:
        h_in[m].wait()

        def pack_head(z, packed):
            return pack(0, m, z, hb[m, z, PAD : PAD + yb, :], packed)

        send_edges(0, m, lax.fori_loop(0, nz, pack_head, (zero, zero), unroll=True))

    def wait_all(ref, sem):
        pltpu.make_async_copy(ref, ref, sem).wait()

    def copy2(m, half, to):
        return pltpu.make_async_remote_copy(
            src_ref=yo.at[m, pl.ds(blocks_of(gx, gy, to, j, half), 2)],
            dst_ref=r2.at[m, half, i],
            send_sem=s2.at[m, half],
            recv_sem=v2.at[m, half],
            device_id=(to, j),
            device_id_type=MESH,
        )

    def filter_y(m):
        per = 256 // yb
        for s in range(gy):
            high, low = split(r1[m, s])
            bcat[s * yb : (s + 1) * yb, 0:xb] = high
            bcat[s * yb : (s + 1) * yb, xb : 2 * xb] = low
        for turn in range(2):
            half = (j + turn) % 2
            for start, takers in chunks_of(gx, gy, j, half):
                lines = pl.ds(pl.multiple_of(start * yb, 256), 256)
                p = dot(c_v[0, lines, :], bcat[...])
                r = p[:, :xb] + p[:, xb:] + dot(c_v[1, lines, :], bcat[:, 0:xb])
                yo[m, pl.ds(start, per)] = r.reshape(per, yb, xb)
                for to in takers:

                    @pl.when(to != i)
                    def _():
                        copy2(m, half, to).start()

            r2[m, half, i] = yo[m, pl.ds(blocks_of(gx, gy, i, j, half), 2)]

    def copy3(m, half, to, c):
        return pltpu.make_async_remote_copy(
            src_ref=xo.at[m, half, to, c],
            dst_ref=lk.at[m, j],
            send_sem=s3.at[m],
            recv_sem=v3.at[m],
            device_id=(to, blocks_of(gx, gy, i, j, half) + c),
            device_id_type=MESH,
        )

    def each3(m, half, to, here, there):
        for c in range(2):
            own = (to == i) & (blocks_of(gx, gy, i, j, half) + c == j)

            @pl.when(own)
            def _():
                here(m, half, to, c)

            @pl.when(jnp.logical_not(own))
            def _():
                there(m, half, to, c)

    def keep3(m, half, to, c):
        pltpu.make_async_copy(xo.at[m, half, to, c], lk.at[m, j], v3.at[m]).start()

    def filter_x(m):
        for turn in range(2):
            half = (j + turn) % 2
            wait_all(r2.at[m, half, pl.ds(0, gx - 1)], v2.at[m, half])
            for s in range(gx):
                high, low = split(r2[m, half, s].reshape(rows, xb))
                acat[0:rows, s * xb : (s + 1) * xb] = high
                acat[rows : 2 * rows, s * xb : (s + 1) * xb] = low
            for turn_x in range(gx // 2):
                pair = (i // 2 + turn_x) % (gx // 2)
                cols = pl.ds(pl.multiple_of(pair * 2 * xb, 2 * xb), 2 * xb)
                p = dot(acat[...], c_v[0, :, cols])
                r = p[:rows] + p[rows:] + dot(acat[0:rows, :], c_v[1, :, cols])
                for side in range(2):
                    to = 2 * pair + side
                    xo[m, half, to] = r[:, side * xb : (side + 1) * xb].reshape(2, yb, xb)
                    each3(m, half, to, keep3, lambda *at: copy3(*at).start())

    c_in.wait()
    for m in members:
        wait_all(r1.at[m, pl.ds(0, gy - 1)], v1.at[m])
        filter_y(m)
        filter_x(m)

    row_at = yb * j + lax.broadcasted_iota(jnp.int32, (yb, xb), 0)
    col_at = xb * i + lane
    pinned = (row_at == 0) | (row_at == n - 1) | (col_at == 0) | (col_at == n - 1)

    def inverse(x):
        guess = pl.reciprocal(x, approx=True)
        return guess * (2.0 - x * guess)

    def layer(ref, m, z):
        return ref[m, z, PAD : PAD + yb, :]

    def above(ref, m, z):
        return ref[m, z, PAD - 1 : PAD - 1 + yb, :]

    def under(ref, m, z):
        return ref[m, z, PAD + 1 : PAD + 1 + yb, :]

    def to_lane(packed, z):
        return pltpu.roll(packed, (xb - 2 * z) % xb, 1)

    def flow_x(w_left, w_right, h, edge, z):
        e = to_lane(edge, z)
        h_right = jnp.where(last, e, pltpu.roll(h, xb - 1, 1))
        h_left = jnp.where(first, e, pltpu.roll(h, 1, 1))
        return w_right * h_right + w_left * h_left

    def resist(m):
        wait_all(lk.at[m], v3.at[m])
        pltpu.make_async_copy(lk.at[m], lk_hbm.at[m], out_sem.at[m]).start()

        def step(z, packed):
            r = jnp.exp(-lk[m, z])
            rb[m, z, PAD : PAD + yb, :] = r
            return pack(1, m, z, r, packed)

        send_edges(1, m, lax.fori_loop(0, nz, step, (zero, zero), unroll=True))
        for z in (0, nz - 1):
            gb[m, z, PAD : PAD + yb, :] = layer(hb, m, z)
            ho[m, z] = layer(hb, m, z)

    row_of = lax.broadcasted_iota(jnp.int32, (yb, xb), 0)
    z_of = lax.broadcasted_iota(jnp.int32, (nz, xb), 0)
    z_lane = lax.broadcasted_iota(jnp.int32, (nz, xb), 1)
    z_col = xb * i + z_lane
    row_pinned = (z_of == 0) | (z_of == nz - 1) | (z_col == 0) | (z_col == n - 1)
    top = 2 * nz - 2
    col_pinned = (row_at == 0) | (row_at == n - 1) | first | last | (lane == top) | (lane == top - 1)

    def relaxed(r, h, pairs, kept):
        weights = [inverse(r + r_beside) for r_beside, _ in pairs]
        total = sum(weights[1:], weights[0])
        gain = sum(w * h_beside for w, (_, h_beside) in zip(weights, pairs))
        return jnp.where(kept, h, gain * inverse(total))

    def ring(m, r_edges, h_edges):
        def along_rows(edges, field, side):
            beside, beyond = row_in[field, m, 1 - side, 0], row_in[field, m, 1 - side, 1]
            corners = edges[3 + side]
            pick = lambda at: jnp.sum(jnp.where(z_lane == at, corners, 0.0), axis=1, keepdims=True)
            left, right = pick(2 * z_of), pick((2 * z_of + xb - 1) % xb)
            return beside, (
                beyond,
                row_out[field, m, side, 0],
                jnp.where(z_lane == 0, left, pltpu.roll(beside, 1, 1)),
                jnp.where(z_lane == xb - 1, right, pltpu.roll(beside, xb - 1, 1)),
                pltpu.roll(beside, 1, 0),
                pltpu.roll(beside, nz - 1, 0),
            )

        for side in range(2):
            r, r_pairs = along_rows(r_edges, 1, side)
            h, h_pairs = along_rows(h_edges, 0, side)
            new = relaxed(r, h, list(zip(r_pairs, h_pairs)), row_pinned)
            at = (PAD - 1, PAD + yb)[side]
            for z in range(nz):
                gb[m, z, at : at + 1, :] = new[z : z + 1]

        def along_cols(edges):
            beside, beyond, own, up, down = edges
            return beside, (
                beyond,
                own,
                jnp.where(row_of == 0, up, pltpu.roll(beside, 1, 0)),
                jnp.where(row_of == yb - 1, down, pltpu.roll(beside, yb - 1, 0)),
                pltpu.roll(beside, 2, 1),
                pltpu.roll(beside, xb - 2, 1),
            )

        r, r_pairs = along_cols(r_edges)
        h, h_pairs = along_cols(h_edges)
        return relaxed(r, h, list(zip(r_pairs, h_pairs)), col_pinned)

    def sweeps(m):
        h_edges = take_edges(0, hb, m)
        r_edges = take_edges(1, rb, m)
        h_edge = h_edges[0]
        w_edge = inverse(r_edges[2] + r_edges[0])
        g_edge = ring(m, r_edges, h_edges)

        def step(z, carry):
            r, h_low, h, w_low = carry
            r_high = layer(rb, m, z + 1)
            h_high = layer(hb, m, z + 1)
            w_high = inverse(r + r_high)
            w_up = inverse(r + above(rb, m, z))
            w_down = inverse(r + under(rb, m, z))
            w_x = inverse(r + pltpu.roll(r, xb - 1, 1))
            w_end = to_lane(w_edge, z)
            w_left = jnp.where(first, w_end, pltpu.roll(w_x, 1, 1))
            w_right = jnp.where(last, w_end, w_x)
            gain = flow_x(w_left, w_right, h, h_edge, z)
            total = (w_left + w_right) + ((w_low + w_high) + (w_up + w_down))
            gain = gain + (w_low * h_low + w_high * h_high)
            gain = gain + (w_up * above(hb, m, z) + w_down * under(hb, m, z))
            share = inverse(total)
            gb[m, z, PAD : PAD + yb, :] = jnp.where(pinned, h, gain * share)
            wt[0, z] = w_left
            wt[5, z] = w_right
            wt[1, z] = w_high
            wt[2, z] = w_up
            wt[3, z] = w_down
            wt[4, z] = share
            return r_high, h, h_high, w_high

        r0, r1_ = layer(rb, m, 0), layer(rb, m, 1)
        w_first = inverse(r0 + r1_)
        start = (r1_, layer(hb, m, 0), layer(hb, m, 1), w_first)
        lax.fori_loop(1, nz - 1, step, start, unroll=6)

        def again(z, carry):
            h_low, h, w_low = carry
            h_high = layer(gb, m, z + 1)
            w_high = wt[1, z]
            gain = flow_x(wt[0, z], wt[5, z], h, g_edge, z)
            gain = gain + (w_low * h_low + w_high * h_high)
            gain = gain + (wt[2, z] * above(gb, m, z) + wt[3, z] * under(gb, m, z))
            ho[m, z] = jnp.where(pinned, h, gain * wt[4, z])
            return h, h_high, w_high

        start = (layer(gb, m, 0), layer(gb, m, 1), w_first)
        lax.fori_loop(1, nz - 1, again, start, unroll=10)
        pltpu.make_async_copy(ho.at[m], ho_hbm.at[m], out_sem.at[2 + m]).start()

    for m in members:
        resist(m)
    for m in members:
        sweeps(m)

    @pl.loop(1, gy)
    def _(k):
        copy1(1, k).wait_send()

    for m in members:
        pltpu.make_async_copy(lk.at[m], lk_hbm.at[m], out_sem.at[m]).wait()
        pltpu.make_async_copy(ho.at[m], ho_hbm.at[m], out_sem.at[2 + m]).wait()
        for field in range(2):
            for at in range(8):
                edge_copy(field, m, at).wait_send()

        for half in range(2):

            @pl.loop(1, gx)
            def _(k):
                copy2(m, half, (i + k) % gx).wait_send()

            @pl.loop(0, gx)
            def _(to):
                each3(m, half, to, lambda *at: None, lambda *at: copy3(*at).wait_send())


def on_device(gx, gy, white_noise, head_start):
    _, nz, yb, xb = white_noise.shape
    n = yb * gy
    assert n == xb * gx
    assert n == 4 * yb * gx and nz == gy
    rows = 2 * yb
    wide = yb + 2 * PAD
    matrix = jnp.asarray(split_pair(circulant(n)))
    z_matrix = jnp.asarray(split_pair(np.kron(circulant(nz), np.eye(8))))
    block = jax.ShapeDtypeStruct(white_noise.shape, F32)
    dma = pltpu.SemaphoreType.DMA
    results = pl.pallas_call(
        functools.partial(body, gx, gy, n, nz, yb, xb),
        out_shape=(pltpu.VMEM(block.shape, F32),) * 2,
        in_specs=[pl.BlockSpec(memory_space=pl.ANY)] * 4,
        out_specs=(pl.BlockSpec(memory_space=pl.ANY),) * 2,
        scratch_shapes=[
            pltpu.VMEM((2, nz, yb, xb), F32),
            pltpu.VMEM((2, n, n), BF16),
            pltpu.VMEM((2, nz * 8, nz * 8), BF16),
            pltpu.VMEM((2, nz, yb, xb), F32),
            pltpu.VMEM((2, gy, yb, xb), F32),
            pltpu.VMEM((n, 2 * xb), BF16),
            pltpu.VMEM((2, gy, yb, xb), F32),
            pltpu.VMEM((2, 2, gx, 2, yb, xb), F32),
            pltpu.VMEM((2 * rows, n), BF16),
            pltpu.VMEM((2, 2, gx, 2, yb, xb), F32),
            pltpu.VMEM((2, nz, yb, xb), F32),
            pltpu.VMEM((2, nz, wide, xb), F32),
            pltpu.VMEM((2, nz, wide, xb), F32),
            pltpu.VMEM((2, nz, wide, xb), F32),
            pltpu.VMEM((6, nz, yb, xb), F32),
            pltpu.VMEM((2, nz, yb, xb), F32),
            pltpu.VMEM((2, 2, 2, 2, nz, xb), F32),
            pltpu.VMEM((2, 2, 2, 2, nz, xb), F32),
            pltpu.VMEM((2, 2, 2, yb, xb), F32),
            pltpu.VMEM((2, 2, 2, 2, yb, xb), F32),
            pltpu.VMEM((2, 2, 4, 8, xb), F32),
            dma((4,)),
            dma((2,)),
            dma((2,)), dma((2,)),
            dma((2, 2)), dma((2, 2)),
            dma((2,)), dma((2,)),
            dma((2, 2, 8)), dma((2, 2, 8)),
            dma((4,)),
        ],
        compiler_params=pltpu.CompilerParams(
            collective_id=0, has_side_effects=True, vmem_limit_bytes=60 * 1024 * 1024
        ),
        cost_estimate=pl.CostEstimate(
            flops=12 * 2 * rows * 2 * n * n, bytes_accessed=16 * n * xb * 4, transcendentals=2 * nz * yb * xb
        ),
    )(white_noise, head_start, matrix, z_matrix)
    return results


def solution(mesh):
    spec = P(None, None, "gy", "gx")
    return jax.shard_map(
        functools.partial(on_device, mesh.shape["gx"], mesh.shape["gy"]),
        mesh=mesh,
        in_specs=(spec, spec),
        out_specs=(spec, spec),
        check_vma=False,
    )
```

```python
import functools
import math

import jax
import jax.numpy as jnp
import ml_dtypes
import numpy as np
from jax import lax
from jax.experimental import pallas as pl
from jax.experimental.pallas import tpu as pltpu
from jax.sharding import PartitionSpec as P

F32 = jnp.float32
BF16 = jnp.bfloat16
MESH = pl.DeviceIdType.MESH
PAD = 8


def circulant(length):
    k = np.arange(length)
    q = np.minimum(k, length - k)
    w = 2.0 * math.pi * q / length
    s = 1.0 / (1.0 + (w * (length / 16.0)) ** 2)
    a = np.sqrt(s / np.mean(s))
    taps = np.real(np.fft.ifft(a))
    return taps[(k[:, None] - k[None, :]) % length]


def split_pair(matrix):
    high = matrix.astype(ml_dtypes.bfloat16)
    low = (matrix - high.astype(np.float64)).astype(ml_dtypes.bfloat16)
    return np.stack([high, low])


def split(x):
    high = x.astype(BF16)
    low = (x - high.astype(F32)).astype(BF16)
    return high, low


def dot(a, b):
    return jnp.dot(a, b, preferred_element_type=F32)


def blocks_of(gx, gy, i, j, half):
    if (gx, gy) == (8, 32):
        core, z, y_lo = j % 2, (j // 2) % 8, j // 16
        x, y_hi = i % 4, i // 4
        turn = x + 2 * core * x
        return (y_lo + y_hi) % 2 * 16 + (z + turn) % 4 * 2 + 8 * half
    return gy // gx * i + 2 * half


def chunks_of(gx, gy, j, half):
    if (gx, gy) == (8, 32):
        y_lo = j // 16
        return [((y_lo + y_hi) % 2 * 16 + 8 * half, range(4 * y_hi, 4 * y_hi + 4)) for y_hi in range(2)]
    return [(0, range(gx))]


def body(
    gx, gy, n, nz, yb, xb,
    w_hbm, h_hbm, c_hbm, kz_hbm, lk_hbm, ho_hbm,
    w_v, c_v, kz_v, zc, r1, bcat, yo, r2, acat, xo, lk,
    hb, rb, gb, wt, ho, row_out, row_in, cols, col_in, corner_in,
    in_sem, c_sem, s1, v1, s2, v2, s3, v3, hs, hv, out_sem,
):
    i = lax.axis_index("gx")
    j = lax.axis_index("gy")
    wide = yb + 2 * PAD
    rows = 2 * yb
    members = range(2)

    w_in = [pltpu.make_async_copy(w_hbm.at[m], w_v.at[m], in_sem.at[m]) for m in members]
    h_in = [
        pltpu.make_async_copy(
            h_hbm.at[m], hb.at[m, :, pl.ds(PAD, yb)], in_sem.at[2 + m]
        )
        for m in members
    ]
    kz_in = pltpu.make_async_copy(kz_hbm, kz_v, c_sem.at[0])
    c_in = pltpu.make_async_copy(c_hbm, c_v, c_sem.at[1])
    kz_in.start()
    w_in[0].start()

    barrier = pltpu.get_barrier_semaphore()

    @pl.loop(1, gx)
    def _(k):
        pl.semaphore_signal(barrier, inc=1, device_id=((i + k) % gx, j), device_id_type=MESH)

    @pl.loop(1, gy)
    def _(k):
        pl.semaphore_signal(barrier, inc=1, device_id=(i, (j + k) % gy), device_id_type=MESH)

    diagonal = [((i + (gx - 1, 1)[cs]) % gx, (j + (gy - 1, 1)[rs]) % gy) for cs in range(2) for rs in range(2)]
    for peer in diagonal:
        pl.semaphore_signal(barrier, inc=1, device_id=peer, device_id_type=MESH)

    w_in[1].start()
    h_in[0].start()
    h_in[1].start()
    c_in.start()

    def filter_z(m):
        for q in range(yb // 8):
            x = w_v[m, :, 8 * q : 8 * q + 8, :].reshape(nz * 8, xb)
            high, low = split(x)
            p = dot(kz_v[0], jnp.concatenate([high, low], axis=1))
            r = p[:, :xb] + p[:, xb:] + dot(kz_v[1], high)
            zc[m, :, 8 * q : 8 * q + 8, :] = r.reshape(nz, 8, xb)
        r1[m, j] = zc[m, j]

    def copy1(m, k):
        peer = (j + k) % gy
        return pltpu.make_async_remote_copy(
            src_ref=zc.at[m, peer],
            dst_ref=r1.at[m, j],
            send_sem=s1.at[m],
            recv_sem=v1.at[m],
            device_id=(i, peer),
            device_id_type=MESH,
        )

    def send1(m, start, end):
        @pl.loop(start, end)
        def _(k):
            copy1(m, k).start()

    kz_in.wait()
    w_in[0].wait()
    filter_z(0)
    pl.semaphore_wait(barrier, gx + gy + 2)
    send1(0, 1, gy)
    w_in[1].wait()
    filter_z(1)

    lane = lax.broadcasted_iota(jnp.int32, (yb, xb), 1)
    first, last = lane == 0, lane == xb - 1
    even = lane % 2 == 0
    layer_0 = lane // 2
    layer_1 = jnp.where(even, lane // 2 - 1, (lane + 1) % xb // 2)
    around = (
        ((i + gx - 1) % gx, j),
        ((i + 1) % gx, j),
        (i, (j + gy - 1) % gy),
        (i, (j + 1) % gy),
        *diagonal,
    )

    def edge_copy(field, m, at):
        if at < 2:
            source, target = cols.at[field, m], col_in.at[field, m, at]
        elif at < 4:
            source, target = row_out.at[field, m, at - 2], row_in.at[field, m, at - 2]
        else:
            start = (0, yb - 8)[at % 2]
            source = cols.at[field, m, 0, pl.ds(start, 8)]
            target = corner_in.at[field, m, at - 4]
        return pltpu.make_async_remote_copy(
            src_ref=source,
            dst_ref=target,
            send_sem=hs.at[field, m, at],
            recv_sem=hv.at[field, m, at],
            device_id=around[at],
            device_id_type=MESH,
        )

    zero = jnp.zeros((yb, xb), F32)

    def pack(field, m, z, x, packed):
        for side, at in enumerate((0, yb - 1)):
            inner = (1, yb - 2)[side]
            row_out[field, m, side, 0, pl.ds(z, 1), :] = x[at : at + 1]
            row_out[field, m, side, 1, pl.ds(z, 1), :] = x[inner : inner + 1]
        turned = pltpu.roll(x, 2 * z + 1, 1)
        return (
            jnp.where(layer_0 == z, turned, packed[0]),
            jnp.where(layer_1 == z, turned, packed[1]),
        )

    def send_edges(field, m, packed):
        cols[field, m, 0] = packed[0]
        cols[field, m, 1] = packed[1]
        for at in range(8):
            edge_copy(field, m, at).start()

    def to_left(x, by):
        return pltpu.roll(x, x.shape[1] - by, 1)

    def take_edges(field, ref, m):
        for at in range(8):
            edge_copy(field, m, at).wait_recv()
        if ref is not None:
            for z in range(nz):
                ref[m, z, PAD + yb : PAD + yb + 1, :] = row_in[field, m, 0, 0, z : z + 1, :]
                ref[m, z, PAD - 1 : PAD, :] = row_in[field, m, 1, 0, z : z + 1, :]
        beside = jnp.where(even, col_in[field, m, 1, 0], to_left(col_in[field, m, 0, 0], 2))
        beyond = jnp.where(
            even, pltpu.roll(col_in[field, m, 1, 1], 1, 1), to_left(col_in[field, m, 0, 1], 3)
        )
        own = to_left(cols[field, m, 0], 1)
        tile_even = even[0:8]

        def corner(rs, at):
            left, right = corner_in[field, m, 2 + rs], to_left(corner_in[field, m, rs], 2)
            return jnp.where(tile_even, left, right)[at : at + 1]

        return beside, beyond, own, corner(1, 7), corner(0, 0)

    for m in members:
        h_in[m].wait()

        def pack_head(z, packed):
            return pack(0, m, z, hb[m, z, PAD : PAD + yb, :], packed)

        send_edges(0, m, lax.fori_loop(0, nz, pack_head, (zero, zero), unroll=True))

    @pl.loop(1, gy)
    def _(k):
        copy1(0, k).wait_send()

    send1(1, 1, gy)

    def wait_all(ref, sem):
        pltpu.make_async_copy(ref, ref, sem).wait()

    def copy2(m, half, to):
        return pltpu.make_async_remote_copy(
            src_ref=yo.at[m, pl.ds(blocks_of(gx, gy, to, j, half), 2)],
            dst_ref=r2.at[m, half, i],
            send_sem=s2.at[m, half],
            recv_sem=v2.at[m, half],
            device_id=(to, j),
            device_id_type=MESH,
        )

    def filter_y(m):
        wait_all(r1.at[m, pl.ds(0, gy - 1)], v1.at[m])
        per = 256 // yb
        for s in range(gy):
            high, low = split(r1[m, s])
            bcat[s * yb : (s + 1) * yb, 0:xb] = high
            bcat[s * yb : (s + 1) * yb, xb : 2 * xb] = low
        for turn in range(2):
            half = (j + turn) % 2
            for start, takers in chunks_of(gx, gy, j, half):
                lines = pl.ds(pl.multiple_of(start * yb, 256), 256)
                p = dot(c_v[0, lines, :], bcat[...])
                r = p[:, :xb] + p[:, xb:] + dot(c_v[1, lines, :], bcat[:, 0:xb])
                yo[m, pl.ds(start, per)] = r.reshape(per, yb, xb)
                for to in takers:

                    @pl.when(to != i)
                    def _():
                        copy2(m, half, to).start()

            r2[m, half, i] = yo[m, pl.ds(blocks_of(gx, gy, i, j, half), 2)]

    def copy3(m, half, to, c):
        return pltpu.make_async_remote_copy(
            src_ref=xo.at[m, half, to, c],
            dst_ref=lk.at[m, j],
            send_sem=s3.at[m],
            recv_sem=v3.at[m],
            device_id=(to, blocks_of(gx, gy, i, j, half) + c),
            device_id_type=MESH,
        )

    def each3(m, half, to, here, there):
        for c in range(2):
            own = (to == i) & (blocks_of(gx, gy, i, j, half) + c == j)

            @pl.when(own)
            def _():
                here(m, half, to, c)

            @pl.when(jnp.logical_not(own))
            def _():
                there(m, half, to, c)

    def keep3(m, half, to, c):
        pltpu.make_async_copy(xo.at[m, half, to, c], lk.at[m, j], v3.at[m]).start()

    def filter_x(m, turns):
        for turn in turns:
            half = (j + turn) % 2
            wait_all(r2.at[m, half, pl.ds(0, gx - 1)], v2.at[m, half])
            for s in range(gx):
                high, low = split(r2[m, half, s].reshape(rows, xb))
                acat[0:rows, s * xb : (s + 1) * xb] = high
                acat[rows : 2 * rows, s * xb : (s + 1) * xb] = low
            for turn_x in range(gx // 2):
                pair = (i // 2 + turn_x) % (gx // 2)
                cols = pl.ds(pl.multiple_of(pair * 2 * xb, 2 * xb), 2 * xb)
                p = dot(acat[...], c_v[0, :, cols])
                r = p[:rows] + p[rows:] + dot(acat[0:rows, :], c_v[1, :, cols])
                for side in range(2):
                    to = 2 * pair + side
                    xo[m, half, to] = r[:, side * xb : (side + 1) * xb].reshape(2, yb, xb)
                    each3(m, half, to, keep3, lambda *at: copy3(*at).start())

    c_in.wait()
    filter_y(0)
    filter_x(0, (0,))
    filter_y(1)
    filter_x(0, (1,))
    filter_x(1, (0, 1))

    row_at = yb * j + lax.broadcasted_iota(jnp.int32, (yb, xb), 0)
    col_at = xb * i + lane
    pinned = (row_at == 0) | (row_at == n - 1) | (col_at == 0) | (col_at == n - 1)

    def inverse(x):
        guess = pl.reciprocal(x, approx=True)
        return guess * (2.0 - x * guess)

    def layer(ref, m, z):
        return ref[m, z, PAD : PAD + yb, :]

    def above(ref, m, z):
        return ref[m, z, PAD - 1 : PAD - 1 + yb, :]

    def under(ref, m, z):
        return ref[m, z, PAD + 1 : PAD + 1 + yb, :]

    def to_lane(packed, z):
        return pltpu.roll(packed, (xb - 2 * z) % xb, 1)

    def flow_x(w_left, w_right, h, edge, z):
        e = to_lane(edge, z)
        h_right = jnp.where(last, e, pltpu.roll(h, xb - 1, 1))
        h_left = jnp.where(first, e, pltpu.roll(h, 1, 1))
        return w_right * h_right + w_left * h_left

    def resist(m):
        wait_all(lk.at[m], v3.at[m])
        pltpu.make_async_copy(lk.at[m], lk_hbm.at[m], out_sem.at[m]).start()

        def step(z, packed):
            r = jnp.exp(-lk[m, z])
            rb[m, z, PAD : PAD + yb, :] = r
            return pack(1, m, z, r, packed)

        send_edges(1, m, lax.fori_loop(0, nz, step, (zero, zero), unroll=True))
        for z in (0, nz - 1):
            gb[m, z, PAD : PAD + yb, :] = layer(hb, m, z)
            ho[m, z] = layer(hb, m, z)

    row_of = lax.broadcasted_iota(jnp.int32, (yb, xb), 0)
    z_of = lax.broadcasted_iota(jnp.int32, (nz, xb), 0)
    z_lane = lax.broadcasted_iota(jnp.int32, (nz, xb), 1)
    z_col = xb * i + z_lane
    row_pinned = (z_of == 0) | (z_of == nz - 1) | (z_col == 0) | (z_col == n - 1)
    top = 2 * nz - 2
    col_pinned = (row_at == 0) | (row_at == n - 1) | first | last | (lane == top) | (lane == top - 1)

    def relaxed(r, h, pairs, kept):
        weights = [inverse(r + r_beside) for r_beside, _ in pairs]
        total = sum(weights[1:], weights[0])
        gain = sum(w * h_beside for w, (_, h_beside) in zip(weights, pairs))
        return jnp.where(kept, h, gain * inverse(total))

    def ring(m, r_edges, h_edges):
        def along_rows(edges, field, side):
            beside, beyond = row_in[field, m, 1 - side, 0], row_in[field, m, 1 - side, 1]
            corners = edges[3 + side]
            pick = lambda at: jnp.sum(jnp.where(z_lane == at, corners, 0.0), axis=1, keepdims=True)
            left, right = pick(2 * z_of), pick((2 * z_of + xb - 1) % xb)
            return beside, (
                beyond,
                row_out[field, m, side, 0],
                jnp.where(z_lane == 0, left, pltpu.roll(beside, 1, 1)),
                jnp.where(z_lane == xb - 1, right, pltpu.roll(beside, xb - 1, 1)),
                pltpu.roll(beside, 1, 0),
                pltpu.roll(beside, nz - 1, 0),
            )

        for side in range(2):
            r, r_pairs = along_rows(r_edges, 1, side)
            h, h_pairs = along_rows(h_edges, 0, side)
            new = relaxed(r, h, list(zip(r_pairs, h_pairs)), row_pinned)
            at = (PAD - 1, PAD + yb)[side]
            for z in range(nz):
                gb[m, z, at : at + 1, :] = new[z : z + 1]

        def along_cols(edges):
            beside, beyond, own, up, down = edges
            return beside, (
                beyond,
                own,
                jnp.where(row_of == 0, up, pltpu.roll(beside, 1, 0)),
                jnp.where(row_of == yb - 1, down, pltpu.roll(beside, yb - 1, 0)),
                pltpu.roll(beside, 2, 1),
                pltpu.roll(beside, xb - 2, 1),
            )

        r, r_pairs = along_cols(r_edges)
        h, h_pairs = along_cols(h_edges)
        return relaxed(r, h, list(zip(r_pairs, h_pairs)), col_pinned)

    def sweeps(m):
        h_edges = take_edges(0, hb, m)
        r_edges = take_edges(1, rb, m)
        h_edge = h_edges[0]
        w_edge = inverse(r_edges[2] + r_edges[0])
        g_edge = ring(m, r_edges, h_edges)

        def step(z, carry):
            r, h_low, h, w_low = carry
            r_high = layer(rb, m, z + 1)
            h_high = layer(hb, m, z + 1)
            w_high = inverse(r + r_high)
            w_up = inverse(r + above(rb, m, z))
            w_down = inverse(r + under(rb, m, z))
            w_x = inverse(r + pltpu.roll(r, xb - 1, 1))
            w_end = to_lane(w_edge, z)
            w_left = jnp.where(first, w_end, pltpu.roll(w_x, 1, 1))
            w_right = jnp.where(last, w_end, w_x)
            gain = flow_x(w_left, w_right, h, h_edge, z)
            total = (w_left + w_right) + ((w_low + w_high) + (w_up + w_down))
            gain = gain + (w_low * h_low + w_high * h_high)
            gain = gain + (w_up * above(hb, m, z) + w_down * under(hb, m, z))
            share = inverse(total)
            gb[m, z, PAD : PAD + yb, :] = jnp.where(pinned, h, gain * share)
            wt[0, z] = w_left
            wt[5, z] = w_right
            wt[1, z] = w_high
            wt[2, z] = w_up
            wt[3, z] = w_down
            wt[4, z] = share
            return r_high, h, h_high, w_high

        r0, r1_ = layer(rb, m, 0), layer(rb, m, 1)
        w_first = inverse(r0 + r1_)
        start = (r1_, layer(hb, m, 0), layer(hb, m, 1), w_first)
        lax.fori_loop(1, nz - 1, step, start, unroll=6)

        def again(z, carry):
            h_low, h, w_low = carry
            h_high = layer(gb, m, z + 1)
            w_high = wt[1, z]
            gain = flow_x(wt[0, z], wt[5, z], h, g_edge, z)
            gain = gain + (w_low * h_low + w_high * h_high)
            gain = gain + (wt[2, z] * above(gb, m, z) + wt[3, z] * under(gb, m, z))
            ho[m, z] = jnp.where(pinned, h, gain * wt[4, z])
            return h, h_high, w_high

        start = (layer(gb, m, 0), layer(gb, m, 1), w_first)
        lax.fori_loop(1, nz - 1, again, start, unroll=10)
        pltpu.make_async_copy(ho.at[m], ho_hbm.at[m], out_sem.at[2 + m]).start()

    for m in members:
        resist(m)
    for m in members:
        sweeps(m)

    @pl.loop(1, gy)
    def _(k):
        copy1(1, k).wait_send()

    for m in members:
        pltpu.make_async_copy(lk.at[m], lk_hbm.at[m], out_sem.at[m]).wait()
        pltpu.make_async_copy(ho.at[m], ho_hbm.at[m], out_sem.at[2 + m]).wait()
        for field in range(2):
            for at in range(8):
                edge_copy(field, m, at).wait_send()

        for half in range(2):

            @pl.loop(1, gx)
            def _(k):
                copy2(m, half, (i + k) % gx).wait_send()

            @pl.loop(0, gx)
            def _(to):
                each3(m, half, to, lambda *at: None, lambda *at: copy3(*at).wait_send())


def on_device(gx, gy, white_noise, head_start):
    _, nz, yb, xb = white_noise.shape
    n = yb * gy
    assert n == xb * gx
    assert n == 4 * yb * gx and nz == gy
    rows = 2 * yb
    wide = yb + 2 * PAD
    matrix = jnp.asarray(split_pair(circulant(n)))
    z_matrix = jnp.asarray(split_pair(np.kron(circulant(nz), np.eye(8))))
    block = jax.ShapeDtypeStruct(white_noise.shape, F32)
    dma = pltpu.SemaphoreType.DMA
    results = pl.pallas_call(
        functools.partial(body, gx, gy, n, nz, yb, xb),
        out_shape=(pltpu.VMEM(block.shape, F32),) * 2,
        in_specs=[pl.BlockSpec(memory_space=pl.ANY)] * 4,
        out_specs=(pl.BlockSpec(memory_space=pl.ANY),) * 2,
        scratch_shapes=[
            pltpu.VMEM((2, nz, yb, xb), F32),
            pltpu.VMEM((2, n, n), BF16),
            pltpu.VMEM((2, nz * 8, nz * 8), BF16),
            pltpu.VMEM((2, nz, yb, xb), F32),
            pltpu.VMEM((2, gy, yb, xb), F32),
            pltpu.VMEM((n, 2 * xb), BF16),
            pltpu.VMEM((2, gy, yb, xb), F32),
            pltpu.VMEM((2, 2, gx, 2, yb, xb), F32),
            pltpu.VMEM((2 * rows, n), BF16),
            pltpu.VMEM((2, 2, gx, 2, yb, xb), F32),
            pltpu.VMEM((2, nz, yb, xb), F32),
            pltpu.VMEM((2, nz, wide, xb), F32),
            pltpu.VMEM((2, nz, wide, xb), F32),
            pltpu.VMEM((2, nz, wide, xb), F32),
            pltpu.VMEM((6, nz, yb, xb), F32),
            pltpu.VMEM((2, nz, yb, xb), F32),
            pltpu.VMEM((2, 2, 2, 2, nz, xb), F32),
            pltpu.VMEM((2, 2, 2, 2, nz, xb), F32),
            pltpu.VMEM((2, 2, 2, yb, xb), F32),
            pltpu.VMEM((2, 2, 2, 2, yb, xb), F32),
            pltpu.VMEM((2, 2, 4, 8, xb), F32),
            dma((4,)),
            dma((2,)),
            dma((2,)), dma((2,)),
            dma((2, 2)), dma((2, 2)),
            dma((2,)), dma((2,)),
            dma((2, 2, 8)), dma((2, 2, 8)),
            dma((4,)),
        ],
        compiler_params=pltpu.CompilerParams(
            collective_id=0, has_side_effects=True, vmem_limit_bytes=60 * 1024 * 1024
        ),
        cost_estimate=pl.CostEstimate(
            flops=12 * 2 * rows * 2 * n * n, bytes_accessed=16 * n * xb * 4, transcendentals=2 * nz * yb * xb
        ),
    )(white_noise, head_start, matrix, z_matrix)
    return results


def solution(mesh):
    spec = P(None, None, "gy", "gx")
    return jax.shard_map(
        functools.partial(on_device, mesh.shape["gx"], mesh.shape["gy"]),
        mesh=mesh,
        in_specs=(spec, spec),
        out_specs=(spec, spec),
        check_vma=False,
    )
```
